32 devices in a mesh: dp: 8 (over y, x, core), tensor: 4 (over z).
Axes of the slice: x: 2, y: 2, z: 4, core: 2. Of those that a mesh axis runs over, the one named last changes fastest.
Arguments:
- tokens: bfloat16 [64, 577, 1024], P('dp'), may hold values from -6 to 6
- cotangent: bfloat16 [64, 577, 1024], P('dp'), may hold values from -2.09375 to 2.09375
- qkv_weight: float32 [1024, 3, 1024], P(None, None, 'tensor'), may hold values from -0.1875 to 0.1875
- qv_bias: float32 [2, 1024], P(None, 'tensor'), may hold values from -0.3 to 0.3
- proj_weight: float32 [1024, 1024], P('tensor'), may hold values from -2 to 2
- fc1_weight: float32 [1024, 4096], P(None, 'tensor'), may hold values from -0.1875 to 0.1875
- fc1_bias: float32 [4096], P('tensor'), may hold values from -3 to 3
- fc2_weight: float32 [4096, 1024], P('tensor'), may hold values from -0.25 to 0.25
- norm_gains: float32 [2, 1024], replicated, may hold values from 0.5 to 1.5
- shift_biases: float32 [4, 1024], replicated, may hold values from -1.5 to 1.5
- first_qkv_weight: float32 [1024, 3, 1024], P(None, None, 'tensor'), may hold values from -160 to 160
- first_qv_bias: float32 [2, 1024], P(None, 'tensor'), may hold values from -192 to 192
- first_proj_weight: float32 [1024, 1024], P('tensor'), may hold values from -56 to 56
- first_fc1_weight: float32 [1024, 4096], P(None, 'tensor'), may hold values from -56 to 56
- first_fc1_bias: float32 [4096], P('tensor'), may hold values from -56 to 56
- first_fc2_weight: float32 [4096, 1024], P('tensor'), may hold values from -56 to 56
- first_norm_gains: float32 [2, 1024], replicated, may hold values from -56 to 56
- first_shift_biases: float32 [4, 1024], replicated, may hold values from -56 to 56
- second_qkv_weight: float32 [1024, 3, 1024], P(None, None, 'tensor'), may hold values from 124.632 to 498.528
- second_qv_bias: float32 [2, 1024], P(None, 'tensor'), may hold values from 169.8688 to 679.4752
- second_proj_weight: float32 [1024, 1024], P('tensor'), may hold values from 3.6928 to 14.7712
- second_fc1_weight: float32 [1024, 4096], P(None, 'tensor'), may hold values from 3.6928 to 14.7712
- second_fc1_bias: float32 [4096], P('tensor'), may hold values from 3.6928 to 14.7712
- second_fc2_weight: float32 [4096, 1024], P('tensor'), may hold values from 3.6928 to 14.7712
- second_norm_gains: float32 [2, 1024], replicated, may hold values from 923.2 to 3692.8
- second_shift_biases: float32 [4, 1024], replicated, may hold values from 923.2 to 3692.8
Outputs:
- output: bfloat16 [64, 577, 1024], P('dp')
- grad_tokens: bfloat16 [64, 577, 1024], P('dp')
- grad_qkv_weight: float32 [1024, 3, 1024], P(None, None, 'tensor')
- grad_qv_bias: float32 [2, 1024], P(None, 'tensor')
- grad_proj_weight: float32 [1024, 1024], P('tensor')
- grad_fc1_weight: float32 [1024, 4096], P(None, 'tensor')
- grad_fc1_bias: float32 [4096], P('tensor')
- grad_fc2_weight: float32 [4096, 1024], P('tensor')
- grad_norm_gains: float32 [2, 1024], replicated
- grad_shift_biases: float32 [4, 1024], replicated
- new_qkv_weight: float32 [1024, 3, 1024], P(None, None, 'tensor')
- new_qv_bias: float32 [2, 1024], P(None, 'tensor')
- new_proj_weight: float32 [1024, 1024], P('tensor')
- new_fc1_weight: float32 [1024, 4096], P(None, 'tensor')
- new_fc1_bias: float32 [4096], P('tensor')
- new_fc2_weight: float32 [4096, 1024], P('tensor')
- new_norm_gains: float32 [2, 1024], replicated
- new_shift_biases: float32 [4, 1024], replicated
- new_first_qkv_weight: float32 [1024, 3, 1024], P(None, None, 'tensor')
- new_first_qv_bias: float32 [2, 1024], P(None, 'tensor')
- new_first_proj_weight: float32 [1024, 1024], P('tensor')
- new_first_fc1_weight: float32 [1024, 4096], P(None, 'tensor')
- new_first_fc1_bias: float32 [4096], P('tensor')
- new_first_fc2_weight: float32 [4096, 1024], P('tensor')
- new_first_norm_gains: float32 [2, 1024], replicated
- new_first_shift_biases: float32 [4, 1024], replicated
- new_second_qkv_weight: float32 [1024, 3, 1024], P(None, None, 'tensor')
- new_second_qv_bias: float32 [2, 1024], P(None, 'tensor')
- new_second_proj_weight: float32 [1024, 1024], P('tensor')
- new_second_fc1_weight: float32 [1024, 4096], P(None, 'tensor')
- new_second_fc1_bias: float32 [4096], P('tensor')
- new_second_fc2_weight: float32 [4096, 1024], P('tensor')
- new_second_norm_gains: float32 [2, 1024], replicated
- new_second_shift_biases: float32 [4, 1024], replicated
The draws below stay inside these ranges and needn't reach their ends.
All inputs are finite; a program needn't handle non-finite values.
Results may differ from the reference program's by a relative error of at most 0.024.
Values may be sent and summed in bfloat16 or wider, within the bound.
No kernel may reach another device: no remote copies, remote signals or barrier semaphores. Data moves between devices by JAX's collectives and lax.ppermute only.
A program may use at most 576 MiB of HBM per device.

```python
import math
import jax
import jax.numpy as jnp
from jax import lax

D = 1024
HEADS = 16
HD = 64
FF = 4096
SEQ = 577
STEP = 3
IMAGES = 64
N_TENSOR = 4


def draw_shift_biases(key, part):
    key = jax.random.fold_in(key, 11)
    raw = jax.random.normal(key, (4, D), jnp.float32)
    row_scale = jnp.array([0.05, 0.5, 0.5, 0.5], jnp.float32)[:, None]
    return jnp.clip(raw * row_scale, -1.5, 1.5)


def shard_levels(own_key, extent, split, low, largest):
    level = 1.0
    for axis_at, blocks in split:
        heights = jax.random.uniform(jax.random.fold_in(jax.random.fold_in(own_key, 6), axis_at), (blocks,), jnp.float32, low / len(split), largest / len(split))
        level = level * jnp.repeat(jnp.exp(heights), extent[axis_at] // blocks).reshape((-1,) + (1,) * (len(extent) - 1 - axis_at))
    return level


def normal_values(rng, extent, spread, limit, shards=(), held_as=jnp.bfloat16):
    values = jax.random.normal(rng, extent, jnp.float32) * spread
    if len(shards) > 0:
        values = shard_levels(rng, extent, shards, -0.22, 0.18) * values
    return jnp.clip(values, min=-limit, max=limit).astype(held_as)


def setup_inputs(seed: int = 0) -> dict:
    arg_keys = jax.random.split(jax.random.key(seed), 27)
    tokens = normal_values(arg_keys[0], (IMAGES, SEQ, D), 1.0, 6.0, ((0, 8),))
    cotangent = normal_values(arg_keys[1], (IMAGES, SEQ, D), 0.35, 2.09375, ((0, 8),))
    qkv_weight = normal_values(arg_keys[2], (D, 3, D), D ** -0.5, 0.1875, ((2, 4),), jnp.float32)
    qv_bias = normal_values(arg_keys[3], (2, D), 0.05, 0.3, ((1, 4),), jnp.float32)
    proj_weight = normal_values(arg_keys[4], (D, D), (max(D // 128, 1)) ** -0.5, 2.0, ((0, 4),), jnp.float32)
    fc1_weight = normal_values(arg_keys[5], (D, FF), D ** -0.5, 0.1875, ((1, 4),), jnp.float32)
    fc1_bias = normal_values(arg_keys[6], (FF,), 0.5, 3.0, ((0, 4),), jnp.float32)
    fc2_weight = normal_values(arg_keys[7], (FF, D), (max(FF // 8, 1)) ** -0.5, 0.25, ((0, 4),), jnp.float32)
    norm_gains = jnp.clip(1.0 + 0.1 * jax.random.normal(arg_keys[8], (2, D), jnp.float32), 0.5, 1.5)
    shift_biases = draw_shift_biases(jax.random.fold_in(arg_keys[26], 71), 0)
    first_qkv_weight = normal_values(arg_keys[10], (D, 3, D), (0.135 * (IMAGES * SEQ) ** 0.5), 160.0, ((2, 4),), jnp.float32)
    first_qv_bias = normal_values(arg_keys[11], (2, D), (0.1575 * (IMAGES * SEQ) ** 0.5), 192.0, ((1, 4),), jnp.float32)
    first_proj_weight = normal_values(arg_keys[12], (D, D), (0.045 * (IMAGES * SEQ) ** 0.5), 56.0, ((0, 4),), jnp.float32)
    first_fc1_weight = normal_values(arg_keys[13], (D, FF), (0.045 * (IMAGES * SEQ) ** 0.5), 56.0, ((1, 4),), jnp.float32)
    first_fc1_bias = normal_values(arg_keys[14], (FF,), (0.045 * (IMAGES * SEQ) ** 0.5), 56.0, ((0, 4),), jnp.float32)
    first_fc2_weight = normal_values(arg_keys[15], (FF, D), (0.045 * (IMAGES * SEQ) ** 0.5), 56.0, ((0, 4),), jnp.float32)
    first_norm_gains = normal_values(arg_keys[16], (2, D), (0.045 * (IMAGES * SEQ) ** 0.5), 56.0, (), jnp.float32)
    first_shift_biases = normal_values(arg_keys[17], (4, D), (0.045 * (IMAGES * SEQ) ** 0.5), 56.0, (), jnp.float32)
    second_qkv_weight = jnp.clip(jnp.exp(math.log(498.528) - 1.3862944 * jax.random.uniform(arg_keys[18], (D, 3, D), jnp.float32) ** shard_levels(arg_keys[18], (D, 3, D), ((2, 4),), -0.2, 0.2)), 124.632, 498.528)
    second_qv_bias = jnp.clip(jnp.exp(math.log(679.4752) - 1.3862944 * jax.random.uniform(arg_keys[19], (2, D), jnp.float32) ** shard_levels(arg_keys[19], (2, D), ((1, 4),), -0.2, 0.2)), 169.8688, 679.4752)
    second_proj_weight = jnp.clip(jnp.exp(math.log(14.7712) - 1.3862944 * jax.random.uniform(arg_keys[20], (D, D), jnp.float32) ** shard_levels(arg_keys[20], (D, D), ((0, 4),), -0.2, 0.2)), 3.6928, 14.7712)
    second_fc1_weight = jnp.clip(jnp.exp(math.log(14.7712) - 1.3862944 * jax.random.uniform(arg_keys[21], (D, FF), jnp.float32) ** shard_levels(arg_keys[21], (D, FF), ((1, 4),), -0.2, 0.2)), 3.6928, 14.7712)
    second_fc1_bias = jnp.clip(jnp.exp(math.log(14.7712) - 1.3862944 * jax.random.uniform(arg_keys[22], (FF,), jnp.float32) ** shard_levels(arg_keys[22], (FF,), ((0, 4),), -0.2, 0.2)), 3.6928, 14.7712)
    second_fc2_weight = jnp.clip(jnp.exp(math.log(14.7712) - 1.3862944 * jax.random.uniform(arg_keys[23], (FF, D), jnp.float32) ** shard_levels(arg_keys[23], (FF, D), ((0, 4),), -0.2, 0.2)), 3.6928, 14.7712)
    second_norm_gains = jnp.clip(jnp.exp(jax.random.uniform(arg_keys[24], (2, D), jnp.float32, math.log(923.2), math.log(3692.8))), 923.2, 3692.8)
    second_shift_biases = jnp.clip(jnp.exp(jax.random.uniform(arg_keys[25], (4, D), jnp.float32, math.log(923.2), math.log(3692.8))), 923.2, 3692.8)
    return {"tokens": tokens, "cotangent": cotangent, "qkv_weight": qkv_weight, "qv_bias": qv_bias, "proj_weight": proj_weight, "fc1_weight": fc1_weight, "fc1_bias": fc1_bias, "fc2_weight": fc2_weight, "norm_gains": norm_gains, "shift_biases": shift_biases, "first_qkv_weight": first_qkv_weight, "first_qv_bias": first_qv_bias, "first_proj_weight": first_proj_weight, "first_fc1_weight": first_fc1_weight, "first_fc1_bias": first_fc1_bias, "first_fc2_weight": first_fc2_weight, "first_norm_gains": first_norm_gains, "first_shift_biases": first_shift_biases, "second_qkv_weight": second_qkv_weight, "second_qv_bias": second_qv_bias, "second_proj_weight": second_proj_weight, "second_fc1_weight": second_fc1_weight, "second_fc1_bias": second_fc1_bias, "second_fc2_weight": second_fc2_weight, "second_norm_gains": second_norm_gains, "second_shift_biases": second_shift_biases}


NORM_EPS = 1e-05
BETA_ONE = 0.9
BETA_TWO = 0.999
ADAM_EPS = 1e-08
MATRIX_DECAY = 0.05
SQRT_HALF = 0.7071067811865476
INV_SQRT_TAU = 0.3989422804014327

def layer_norm(values_in, gain_row, shift_row):
    center = values_in - lax.optimization_barrier(jnp.mean(values_in, axis=-1, keepdims=True))
    inv_std = lax.rsqrt(lax.optimization_barrier(jnp.mean(center * center, axis=-1, keepdims=True)) + NORM_EPS)
    normed = center * inv_std
    return (normed, inv_std, normed * gain_row + shift_row)

def norm_back(d_normed, normed, inv_std):
    return inv_std * (d_normed - lax.optimization_barrier(jnp.mean(d_normed, axis=-1, keepdims=True)) - normed * lax.optimization_barrier(jnp.mean(d_normed * normed, axis=-1, keepdims=True)))

def gelu_slope(pre_act):
    normal_cdf = 0.5 * (1.0 + lax.erf(pre_act * SQRT_HALF))
    return normal_cdf + pre_act * jnp.exp(-0.5 * pre_act * pre_act) * INV_SQRT_TAU

def grouped_product(left, right, groups):
    token_count = left.shape[0]
    inner = right.shape[0] // groups
    left_parts = left.reshape(token_count, groups, inner).astype(jnp.float32)
    right_parts = right.reshape(groups, inner, right.shape[1]).astype(jnp.float32)
    partial_terms = jnp.einsum('sgc,gcd->gsd', left_parts, right_parts)
    rounded = lax.optimization_barrier(partial_terms.astype(jnp.bfloat16))
    return lax.optimization_barrier(jnp.sum(rounded.astype(jnp.float32), axis=0))

def adamw(weight_old, moment_one, moment_two, grad_sum, rate_value, decay_value):
    new_one = BETA_ONE * moment_one + (1.0 - BETA_ONE) * grad_sum
    new_two = BETA_TWO * moment_two + (1.0 - BETA_TWO) * grad_sum * grad_sum
    one_hat = new_one / (1.0 - BETA_ONE ** STEP)
    two_hat = new_two / (1.0 - BETA_TWO ** STEP)
    new_weight = weight_old - rate_value * (one_hat / (jnp.sqrt(two_hat) + ADAM_EPS) + decay_value * weight_old)
    return (new_weight, new_one, new_two)

def reference(tokens, cotangent, qkv_weight, qv_bias, proj_weight, fc1_weight, fc1_bias, fc2_weight, norm_gains, shift_biases, first_qkv_weight, first_qv_bias, first_proj_weight, first_fc1_weight, first_fc1_bias, first_fc2_weight, first_norm_gains, first_shift_biases, second_qkv_weight, second_qv_bias, second_proj_weight, second_fc1_weight, second_fc1_bias, second_fc2_weight, second_norm_gains, second_shift_biases):
    groups = N_TENSOR
    qkv_b = qkv_weight.astype(jnp.bfloat16)
    proj_b = proj_weight.astype(jnp.bfloat16)
    fc1_b = fc1_weight.astype(jnp.bfloat16)
    fc2_b = fc2_weight.astype(jnp.bfloat16)
    score_scale = 1.0 / math.sqrt(HD)
    inner = D // groups
    qkv_left = jnp.transpose(qkv_b.reshape(D, 3, groups, inner), (2, 1, 3, 0)).reshape(3 * D, D)

    def scores_of(query, keys):
        return jnp.einsum('qhd,khd->hqk', query.astype(jnp.float32), keys.astype(jnp.float32)) * score_scale

    def one_image(carry, inputs):
        image, cot_image = inputs
        x_float = image.astype(jnp.float32)
        normed1, inv_std1, pre1 = layer_norm(x_float, norm_gains[0], shift_biases[0])
        act1 = pre1.astype(jnp.bfloat16)
        qkv = jnp.dot(act1, qkv_b.reshape(D, 3 * D), preferred_element_type=jnp.float32).reshape(SEQ, 3, D)
        query = (qkv[:, 0] + qv_bias[0]).astype(jnp.bfloat16).reshape(SEQ, HEADS, HD)
        keys = qkv[:, 1].astype(jnp.bfloat16).reshape(SEQ, HEADS, HD)
        values = (qkv[:, 2] + qv_bias[1]).astype(jnp.bfloat16).reshape(SEQ, HEADS, HD)
        scores = scores_of(query, keys)
        row_max = lax.optimization_barrier(jnp.max(scores, axis=-1, keepdims=True))
        log_total = row_max + jnp.log(lax.optimization_barrier(jnp.sum(jnp.exp(scores - row_max), axis=-1, keepdims=True)))
        probs = jnp.exp(scores - log_total).astype(jnp.bfloat16)
        attended = jnp.einsum('hqk,khd->qhd', probs.astype(jnp.float32), values.astype(jnp.float32))
        attended = attended.astype(jnp.bfloat16).reshape(SEQ, D)
        attn_out = grouped_product(attended, proj_b, groups)
        resid = x_float + attn_out + shift_biases[2]
        normed2, inv_std2, pre2 = layer_norm(resid, norm_gains[1], shift_biases[1])
        act2 = pre2.astype(jnp.bfloat16)
        pre_act = jnp.dot(act2, fc1_b, preferred_element_type=jnp.float32) + fc1_bias
        hidden = jax.nn.gelu(pre_act, approximate=False).astype(jnp.bfloat16)
        mlp_out = grouped_product(hidden, fc2_b, groups)
        output = (resid + mlp_out + shift_biases[3]).astype(jnp.bfloat16)
        d_out = cot_image.astype(jnp.float32)
        g_out_bias = lax.optimization_barrier(jnp.sum(d_out, axis=0))
        d_hidden = jnp.dot(cot_image, fc2_b.T, preferred_element_type=jnp.float32)
        g_fc2 = jnp.dot(hidden.T, cot_image, preferred_element_type=jnp.float32)
        d_pre = d_hidden * gelu_slope(pre_act)
        g_fc1_bias = lax.optimization_barrier(jnp.sum(d_pre, axis=0))
        d_pre_b = d_pre.astype(jnp.bfloat16)
        g_fc1 = jnp.dot(act2.T, d_pre_b, preferred_element_type=jnp.float32)
        d_act2 = grouped_product(d_pre_b, fc1_b.T, groups)
        g_gain2 = lax.optimization_barrier(jnp.sum(d_act2 * normed2, axis=0))
        g_shift2 = lax.optimization_barrier(jnp.sum(d_act2, axis=0))
        d_resid = d_out + norm_back(d_act2 * norm_gains[1], normed2, inv_std2)
        g_proj_bias = lax.optimization_barrier(jnp.sum(d_resid, axis=0))
        d_resid_b = d_resid.astype(jnp.bfloat16)
        g_proj = jnp.dot(attended.T, d_resid_b, preferred_element_type=jnp.float32)
        d_att = jnp.dot(d_resid_b, proj_b.T, preferred_element_type=jnp.float32)
        d_att = d_att.astype(jnp.bfloat16).reshape(SEQ, HEADS, HD)
        probs_f = jnp.exp(scores_of(query, keys) - log_total)
        probs_b = probs_f.astype(jnp.bfloat16)
        d_values = jnp.einsum('hqk,qhd->khd', probs_b.astype(jnp.float32), d_att.astype(jnp.float32))
        d_probs = jnp.einsum('qhd,khd->hqk', d_att.astype(jnp.float32), values.astype(jnp.float32))
        delta = lax.optimization_barrier(jnp.sum(probs_f * d_probs, axis=-1, keepdims=True))
        d_scores = (probs_f * (d_probs - delta) * score_scale).astype(jnp.bfloat16)
        d_query = jnp.einsum('hqk,khd->qhd', d_scores.astype(jnp.float32), keys.astype(jnp.float32))
        d_keys = jnp.einsum('hqk,qhd->khd', d_scores.astype(jnp.float32), query.astype(jnp.float32))
        g_qv = jnp.stack([lax.optimization_barrier(jnp.sum(d_query.reshape(SEQ, D), axis=0)), lax.optimization_barrier(jnp.sum(d_values.reshape(SEQ, D), axis=0))])
        d_qkv = jnp.stack([d_query.reshape(SEQ, D), d_keys.reshape(SEQ, D), d_values.reshape(SEQ, D)], axis=1)
        d_qkv = d_qkv.astype(jnp.bfloat16)
        g_qkv = jnp.dot(act1.T, d_qkv.reshape(SEQ, 3 * D), preferred_element_type=jnp.float32).reshape(D, 3, D)
        d_qkv_grouped = jnp.transpose(d_qkv.reshape(SEQ, 3, groups, inner), (0, 2, 1, 3)).reshape(SEQ, 3 * D)
        d_act1 = grouped_product(d_qkv_grouped, qkv_left, groups)
        g_gain1 = lax.optimization_barrier(jnp.sum(d_act1 * normed1, axis=0))
        g_shift1 = lax.optimization_barrier(jnp.sum(d_act1, axis=0))
        d_tokens = (d_resid + norm_back(d_act1 * norm_gains[0], normed1, inv_std1)).astype(jnp.bfloat16)
        terms = (g_qkv, g_qv, g_proj, g_fc1, g_fc1_bias, g_fc2, jnp.stack([g_gain1, g_gain2]), jnp.stack([g_shift1, g_shift2, g_proj_bias, g_out_bias]))
        carry = tuple((total + term for total, term in zip(carry, terms)))
        return (carry, (output, d_tokens))
    start = (jnp.zeros((D, 3, D), jnp.float32), jnp.zeros((2, D), jnp.float32), jnp.zeros((D, D), jnp.float32), jnp.zeros((D, FF), jnp.float32), jnp.zeros((FF,), jnp.float32), jnp.zeros((FF, D), jnp.float32), jnp.zeros((2, D), jnp.float32), jnp.zeros((4, D), jnp.float32))
    grads, (output, grad_tokens) = lax.scan(one_image, start, (tokens, cotangent))
    weights = (qkv_weight, qv_bias, proj_weight, fc1_weight, fc1_bias, fc2_weight, norm_gains, shift_biases)
    firsts = (first_qkv_weight, first_qv_bias, first_proj_weight, first_fc1_weight, first_fc1_bias, first_fc2_weight, first_norm_gains, first_shift_biases)
    seconds = (second_qkv_weight, second_qv_bias, second_proj_weight, second_fc1_weight, second_fc1_bias, second_fc2_weight, second_norm_gains, second_shift_biases)
    rates = (1.2 / math.sqrt(D), 0.6, 0.6 / math.sqrt(max(D // 128, 1)), 0.6 / math.sqrt(D), 0.3, 0.6 / math.sqrt(max(FF // 8, 1)), 3.0, 3.0)
    decays = (MATRIX_DECAY, 0.0, MATRIX_DECAY, MATRIX_DECAY, 0.0, MATRIX_DECAY, 0.0, 0.0)
    updated = []
    for weight_old, moment_one, moment_two, grad_sum, rate_value, decay_value in zip(weights, firsts, seconds, grads, rates, decays):
        updated.append(adamw(weight_old, moment_one, moment_two, grad_sum, rate_value, decay_value))
    return (output, grad_tokens, grads[0], grads[1], grads[2], grads[3], grads[4], grads[5], grads[6], grads[7], updated[0][0], updated[1][0], updated[2][0], updated[3][0], updated[4][0], updated[5][0], updated[6][0], updated[7][0], updated[0][1], updated[1][1], updated[2][1], updated[3][1], updated[4][1], updated[5][1], updated[6][1], updated[7][1], updated[0][2], updated[1][2], updated[2][2], updated[3][2], updated[4][2], updated[5][2], updated[6][2], updated[7][2])
```

```python
import math

import jax
import jax.numpy as jnp
from jax import lax
from jax.experimental import pallas as pl
from jax.experimental.pallas import tpu as pltpu
from jax.sharding import PartitionSpec as P

D = 1024
FF = 4096
STEP = 3


NORM_EPS = 1e-05
BETA_ONE = 0.9
BETA_TWO = 0.999
ADAM_EPS = 1e-08
MATRIX_DECAY = 0.05
SQRT_HALF = 0.7071067811865476
INV_SQRT_TAU = 0.3989422804014327


def layer_norm(values_in, gain_row, shift_row):
    center = values_in - jnp.mean(values_in, axis=-1, keepdims=True)
    inv_std = lax.rsqrt(jnp.mean(center * center, axis=-1, keepdims=True) + NORM_EPS)
    normed = center * inv_std
    return (normed, inv_std, normed * gain_row + shift_row)


def norm_back(d_normed, normed, inv_std):
    return inv_std * (
        d_normed
        - jnp.mean(d_normed, axis=-1, keepdims=True)
        - normed * jnp.mean(d_normed * normed, axis=-1, keepdims=True)
    )


def gelu_slope(pre_act):
    normal_cdf = 0.5 * (1.0 + lax.erf(pre_act * SQRT_HALF))
    return normal_cdf + pre_act * jnp.exp(-0.5 * pre_act * pre_act) * INV_SQRT_TAU


def adamw(weight_old, moment_one, moment_two, grad_sum, rate_value, decay_value):
    new_one = BETA_ONE * moment_one + (1.0 - BETA_ONE) * grad_sum
    new_two = BETA_TWO * moment_two + (1.0 - BETA_TWO) * grad_sum * grad_sum
    one_hat = new_one / (1.0 - BETA_ONE**STEP)
    two_hat = new_two / (1.0 - BETA_TWO**STEP)
    new_weight = weight_old - rate_value * (
        one_hat / (jnp.sqrt(two_hat) + ADAM_EPS) + decay_value * weight_old
    )
    return (new_weight, new_one, new_two)


HD=64
LOG2E=1.4426950408889634
NT=(((1,),(1,)),((),()))
NN=(((1,),(0,)),((),()))
TN=(((0,),(0,)),((),()))

def dot(a,b,dims):
    return lax.dot_general(a,b,dims,preferred_element_type=jnp.float32)

def attn_fwd_kernel(qkv_ref, out_ref):
    seq=qkv_ref.shape[1]
    lane=lax.broadcasted_iota(jnp.int32,(seq,2*HD),1)
    low=lane<HD
    for p in range(2):
        q=qkv_ref[0,:,p*128:(p+1)*128]
        k=qkv_ref[0,:,256+p*128:256+(p+1)*128]
        v=qkv_ref[0,:,512+p*128:512+(p+1)*128]
        outs=[]
        for h in range(2):
            qm=jnp.where(low if h==0 else ~low, q, jnp.zeros_like(q))
            s=dot(qm,k,NT)*(0.125*LOG2E)
            m=jnp.max(s,axis=1,keepdims=True)
            e=jnp.exp2(s-m)
            l=jnp.sum(e,axis=1,keepdims=True)
            o=dot(e.astype(jnp.bfloat16),v,NN)
            outs.append(o/l)
        out_ref[0,:,p*128:(p+1)*128]=jnp.where(low,outs[0],outs[1]).astype(jnp.bfloat16)

def attn_bwd_kernel(qkv_ref, do_ref, dqkv_ref, sums_ref):
    seq=qkv_ref.shape[1]
    lane=lax.broadcasted_iota(jnp.int32,(seq,2*HD),1)
    low=lane<HD
    for p in range(2):
        q=qkv_ref[0,:,p*128:(p+1)*128]
        k=qkv_ref[0,:,256+p*128:256+(p+1)*128]
        v=qkv_ref[0,:,512+p*128:512+(p+1)*128]
        do=do_ref[0,:,p*128:(p+1)*128]
        dqs=[];dks=[];dvs=[]
        for h in range(2):
            sel=low if h==0 else ~low
            km=jnp.where(sel,k,jnp.zeros_like(k))
            vm=jnp.where(sel,v,jnp.zeros_like(v))
            st=dot(km,q,NT)*(0.125*LOG2E)
            m=jnp.max(st,axis=0,keepdims=True)
            e=jnp.exp2(st-m)
            r=1.0/jnp.sum(e,axis=0,keepdims=True)
            pt=e*r
            dp=dot(vm,do,NT)
            delta=jnp.sum(pt*dp,axis=0,keepdims=True)
            ds=(pt*((dp-delta)*0.125)).astype(jnp.bfloat16)
            dvs.append(dot(pt.astype(jnp.bfloat16),do,NN))
            dks.append(dot(ds,q,NN))
            dqs.append(dot(ds,k,TN))
        dq=jnp.where(low,dqs[0],dqs[1]); dk=jnp.where(low,dks[0],dks[1]); dv=jnp.where(low,dvs[0],dvs[1])
        dqkv_ref[0,:,p*128:(p+1)*128]=dq.astype(jnp.bfloat16)
        dqkv_ref[0,:,256+p*128:256+(p+1)*128]=dk.astype(jnp.bfloat16)
        dqkv_ref[0,:,512+p*128:512+(p+1)*128]=dv.astype(jnp.bfloat16)
        sums_ref[0,0,0:1,p*128:(p+1)*128]=jnp.sum(dq,axis=0,keepdims=True)
        sums_ref[0,0,1:2,p*128:(p+1)*128]=jnp.sum(dv,axis=0,keepdims=True)

def attn_fwd(qkv):
    n,seq,w=qkv.shape
    g=w//768
    return pl.pallas_call(attn_fwd_kernel,grid=(n,g),
        in_specs=[pl.BlockSpec((1,seq,768),lambda i,t:(i,0,t))],
        out_specs=pl.BlockSpec((1,seq,256),lambda i,t:(i,0,t)),
        out_shape=jax.ShapeDtypeStruct((n,seq,g*256),jnp.bfloat16),
        compiler_params=pltpu.CompilerParams(vmem_limit_bytes=56*2**20),name="attn_fwd",
        cost_estimate=pl.CostEstimate(flops=n*g*4*4*seq*seq*64*4,bytes_accessed=n*seq*(w+g*256)*2,transcendentals=n*g*4*seq*seq))(qkv)

def attn_bwd(qkv,do):
    n,seq,w=qkv.shape
    g=w//768
    return pl.pallas_call(attn_bwd_kernel,grid=(n,g),
        in_specs=[pl.BlockSpec((1,seq,768),lambda i,t:(i,0,t)),pl.BlockSpec((1,seq,256),lambda i,t:(i,0,t))],
        out_specs=[pl.BlockSpec((1,seq,768),lambda i,t:(i,0,t)),pl.BlockSpec((1,1,2,256),lambda i,t:(i,t,0,0))],
        out_shape=[jax.ShapeDtypeStruct((n,seq,w),jnp.bfloat16),jax.ShapeDtypeStruct((n,g,2,256),jnp.float32)],
        compiler_params=pltpu.CompilerParams(vmem_limit_bytes=56*2**20),name="attn_bwd",
        cost_estimate=pl.CostEstimate(flops=n*g*4*10*seq*seq*64*4,bytes_accessed=n*seq*(w+g*256)*4,transcendentals=n*g*4*seq*seq))(qkv,do)

def matmul(left, right):
    return lax.dot_general(left, right, (((left.ndim - 1,), (0,)), ((), ())), preferred_element_type=jnp.float32)


def matmul_t(left, right):
    return lax.dot_general(left, right, (((left.ndim - 1,), (1,)), ((), ())), preferred_element_type=jnp.float32)


def weight_grad(left, right):
    return lax.dot_general(left, right, (((0, 1), (0, 1)), ((), ())), preferred_element_type=jnp.float32)


def per_device(*args):
    tokens, cotangent = args[0], args[1]
    weights, firsts, seconds = args[2:10], args[10:18], args[18:26]
    qkv_weight, qv_bias, proj_weight, fc1_weight, fc1_bias, fc2_weight, norm_gains, shift_biases = weights
    n_t = lax.axis_size("tensor")
    n_dp = lax.axis_size("dp")
    t_at = lax.axis_index("tensor")
    dp_at = lax.axis_index("dp")
    width = tokens.shape[2]
    own = tokens.shape[0] // n_t
    x = lax.dynamic_slice_in_dim(tokens, t_at * own, own, 0)
    cot = lax.dynamic_slice_in_dim(cotangent, t_at * own, own, 0)

    def full_weight(shard):
        rows = shard.shape[0] // n_dp
        piece = lax.dynamic_slice_in_dim(shard, dp_at * rows, rows, 0).astype(jnp.bfloat16)
        return lax.all_gather(piece, ("tensor", "dp"), axis=0, tiled=True)

    lw = qkv_weight.shape[2]
    qkv_w = full_weight(qkv_weight.reshape(width, 3 * lw)).reshape(n_t, width, 3 * lw)
    proj_w = full_weight(proj_weight)
    fc1_w = full_weight(fc1_weight).reshape(n_t, width, fc1_weight.shape[1])
    fc2_w = full_weight(fc2_weight)
    small = jnp.concatenate([qv_bias.reshape(-1), fc1_bias])
    small = lax.all_gather(small, "tensor", axis=0, tiled=False)
    qv_all = small[:, : 2 * lw].reshape(n_t, 2, lw)
    b1_all = small[:, 2 * lw :].reshape(-1)

    x_float = x.astype(jnp.float32)
    normed1, inv_std1, pre1 = layer_norm(x_float, norm_gains[0], shift_biases[0])
    act1 = pre1.astype(jnp.bfloat16)
    qkv_bias = jnp.stack([qv_all[:, 0], jnp.zeros_like(qv_all[:, 0]), qv_all[:, 1]], axis=1).reshape(n_t, 3 * lw)
    qkv = jnp.concatenate(
        [(matmul(act1, qkv_w[t]) + qkv_bias[t]).astype(jnp.bfloat16) for t in range(n_t)], axis=2
    )
    attended = attn_fwd(qkv)
    resid = x_float + matmul(attended, proj_w) + shift_biases[2]
    normed2, inv_std2, pre2 = layer_norm(resid, norm_gains[1], shift_biases[1])
    act2 = pre2.astype(jnp.bfloat16)
    pre_act = jnp.concatenate([matmul(act2, fc1_w[t]) for t in range(n_t)], axis=2) + b1_all
    normal_cdf = 0.5 * (1.0 + lax.erf(pre_act * SQRT_HALF))
    hidden = (pre_act * normal_cdf).astype(jnp.bfloat16)
    slope = (normal_cdf + pre_act * jnp.exp(-0.5 * pre_act * pre_act) * INV_SQRT_TAU).astype(jnp.bfloat16)
    out_own = (resid + matmul(hidden, fc2_w) + shift_biases[3]).astype(jnp.bfloat16)
    output = lax.all_gather(out_own, "tensor", axis=0, tiled=True)

    def reduce_grad(full):
        rows = full.shape[1] // n_dp
        parts = full.reshape(n_t, n_dp, rows, full.shape[2]).transpose(1, 0, 2, 3).astype(jnp.bfloat16)
        part = lax.psum_scatter(parts, "dp", scatter_dimension=0, tiled=False)
        part = lax.psum_scatter(part, "tensor", scatter_dimension=0, tiled=False)
        return lax.all_gather(part, "dp", axis=0, tiled=True).astype(jnp.float32)

    d_out = cot.astype(jnp.float32)
    g_out_bias = jnp.sum(d_out, axis=(0, 1))
    d_pre = matmul_t(cot, fc2_w) * slope.astype(jnp.float32)
    g_fc1_bias = jnp.sum(d_pre, axis=(0, 1))
    d_pre_b = d_pre.astype(jnp.bfloat16)
    g_fc2 = reduce_grad(weight_grad(hidden, cot).reshape(n_t, -1, width))
    fw = fc1_w.shape[2]
    g_fc1 = reduce_grad(
        jnp.stack([weight_grad(act2, d_pre_b[:, :, t * fw : (t + 1) * fw]) for t in range(n_t)])
    )
    d_act2 = sum(matmul_t(d_pre_b[:, :, t * fw : (t + 1) * fw], fc1_w[t]) for t in range(n_t))
    g_gain2 = jnp.sum(d_act2 * normed2, axis=(0, 1))
    g_shift2 = jnp.sum(d_act2, axis=(0, 1))
    d_resid = d_out + norm_back(d_act2 * norm_gains[1], normed2, inv_std2)
    g_proj_bias = jnp.sum(d_resid, axis=(0, 1))
    d_resid_b = d_resid.astype(jnp.bfloat16)
    g_proj = reduce_grad(weight_grad(attended, d_resid_b).reshape(n_t, -1, width))
    d_att = matmul_t(d_resid_b, proj_w).astype(jnp.bfloat16)
    d_qkv, qkv_sums = attn_bwd(qkv, d_att)
    g_qv = jnp.sum(qkv_sums, axis=0)
    g_qkv = reduce_grad(
        jnp.stack([weight_grad(act1, d_qkv[:, :, t * 3 * lw : (t + 1) * 3 * lw]) for t in range(n_t)])
    ).reshape(width, 3, lw)
    d_act1 = sum(matmul_t(d_qkv[:, :, t * 3 * lw : (t + 1) * 3 * lw], qkv_w[t]) for t in range(n_t))
    g_gain1 = jnp.sum(d_act1 * normed1, axis=(0, 1))
    g_shift1 = jnp.sum(d_act1, axis=(0, 1))
    gt_own = (d_resid + norm_back(d_act1 * norm_gains[0], normed1, inv_std1)).astype(jnp.bfloat16)
    grad_tokens = lax.all_gather(gt_own, "tensor", axis=0, tiled=True)

    vecs = jnp.concatenate(
        [
            g_qv.reshape(-1),
            g_fc1_bias,
            g_gain1,
            g_gain2,
            g_shift1,
            g_shift2,
            g_proj_bias,
            g_out_bias,
        ]
    )
    vecs = lax.psum(vecs, ("dp", "tensor"))
    g_qv = lax.dynamic_index_in_dim(vecs[: 2 * width].reshape(n_t, 2, lw), t_at, 0, keepdims=False)
    g_fc1_bias = lax.dynamic_slice_in_dim(vecs, 2 * width + t_at * fw, fw, 0)
    rest = vecs[2 * width + n_t * fw :].reshape(6, width)
    grads = (g_qkv, g_qv, g_proj, g_fc1, g_fc1_bias, g_fc2, rest[:2], rest[2:])
    rates = (
        1.2 / math.sqrt(D),
        0.6,
        0.6 / math.sqrt(max(D // 128, 1)),
        0.6 / math.sqrt(D),
        0.3,
        0.6 / math.sqrt(max(FF // 8, 1)),
        3.0,
        3.0,
    )
    decays = (MATRIX_DECAY, 0.0, MATRIX_DECAY, MATRIX_DECAY, 0.0, MATRIX_DECAY, 0.0, 0.0)
    updated = [adamw(*leaf) for leaf in zip(weights, firsts, seconds, grads, rates, decays)]
    return (
        output,
        grad_tokens,
        *grads,
        *(u[0] for u in updated),
        *(u[1] for u in updated),
        *(u[2] for u in updated),
    )


def solution(mesh):
    weights = (
        P(None, None, "tensor"),
        P(None, "tensor"),
        P("tensor", None),
        P(None, "tensor"),
        P("tensor"),
        P("tensor", None),
        P(),
        P(),
    )
    images = (P("dp", None, None), P("dp", None, None))
    return jax.shard_map(
        per_device,
        mesh=mesh,
        in_specs=images + weights * 3,
        out_specs=images + weights * 4,
        check_vma=False,
    )
```

```python
import math

import jax
import jax.numpy as jnp
from jax import lax
from jax.experimental import pallas as pl
from jax.experimental.pallas import tpu as pltpu
from jax.sharding import PartitionSpec as P

D = 1024
FF = 4096
STEP = 3
BETA_ONE = 0.9
BETA_TWO = 0.999
ADAM_EPS = 1e-08
MATRIX_DECAY = 0.05

HD=64
LOG2E=1.4426950408889634
NORM_EPS = 1e-05
SQRT_HALF = 0.7071067811865476
INV_SQRT_TAU = 0.3989422804014327
NT=(((1,),(1,)),((),()))
NN=(((1,),(0,)),((),()))
TN=(((0,),(0,)),((),()))
BF=jnp.bfloat16
F32=jnp.float32
VLIM=36*2**20
PAIR=2*HD

def dot(a,b,dims):
    return lax.dot_general(a,b,dims,preferred_element_type=jnp.float32)

def normalize(v):
    center=v-jnp.mean(v,axis=-1,keepdims=True)
    inv_std=lax.rsqrt(jnp.mean(center*center,axis=-1,keepdims=True)+NORM_EPS)
    return center*inv_std,inv_std

def norm_back(d_normed,normed,inv_std):
    return inv_std*(d_normed-jnp.mean(d_normed,axis=-1,keepdims=True)-normed*jnp.mean(d_normed*normed,axis=-1,keepdims=True))

def qkv_attn_kernel(x_ref,gain_ref,shift_ref,w_ref,b_ref,act_ref,qkv_ref,out_ref):
    t=pl.program_id(1)
    @pl.when(t==0)
    def _():
        normed,_=normalize(x_ref[0].astype(F32))
        act_ref[0]=(normed*gain_ref[...]+shift_ref[...]).astype(BF)
    qkv_ref[0]=(dot(act_ref[0],w_ref[0],NN)+b_ref[0]).astype(BF)
    lw=out_ref.shape[2]
    seq=x_ref.shape[1]
    low=lax.broadcasted_iota(jnp.int32,(seq,PAIR),1)<HD
    for p in range(lw//PAIR):
        at=p*PAIR
        q=qkv_ref[0,:,at:at+PAIR]
        k=qkv_ref[0,:,lw+at:lw+at+PAIR]
        v=qkv_ref[0,:,2*lw+at:2*lw+at+PAIR]
        outs=[]
        for sel in (low,~low):
            s=dot(jnp.where(sel,q,jnp.zeros_like(q)),k,NT)*(HD**-0.5*LOG2E)
            e=jnp.exp2(s-jnp.max(s,axis=1,keepdims=True))
            l=jnp.sum(e,axis=1,keepdims=True)
            outs.append(dot(e.astype(BF),v,NN)/l)
        out_ref[0,:,at:at+PAIR]=jnp.where(low,outs[0],outs[1]).astype(BF)

def params(name,flops,nbytes,trans=0,work=1000000):
    return dict(name=name,compiler_params=pltpu.CompilerParams(vmem_limit_bytes=VLIM),
        cost_estimate=pl.CostEstimate(flops=int(work),bytes_accessed=1000000,transcendentals=0))

def row(width): return pl.BlockSpec((1,width),lambda *_:(0,0))

def qkv_attn(at,x,gain,shift,w,b,n=1,work=1000000):
    _,seq,d=x.shape
    g=w.shape[0]
    w3=b.shape[1]
    lw=w3//3
    return pl.pallas_call(qkv_attn_kernel,grid=(n,g),
        in_specs=[pl.BlockSpec((1,seq,d),lambda i,t:(at+i,0,0)),row(d),row(d),
            pl.BlockSpec((1,d,w3),lambda i,t:(t,0,0)),pl.BlockSpec((1,1,w3),lambda i,t:(t,0,0))],
        out_specs=[pl.BlockSpec((1,seq,d),lambda i,t:(i,0,0)),pl.BlockSpec((1,seq,w3),lambda i,t:(i,0,t)),pl.BlockSpec((1,seq,lw),lambda i,t:(i,0,t))],
        out_shape=[jax.ShapeDtypeStruct((n,seq,d),BF),jax.ShapeDtypeStruct((n,seq,g*w3),BF),jax.ShapeDtypeStruct((n,seq,g*lw),BF)],
        **params("qkv_attn",2*n*seq*d*g*w3+16*n*seq*seq*g*lw,n*seq*(2*d+g*w3+g*lw)*2,n*g*lw//HD*seq*seq,work))(x,gain,shift,w,b.reshape(g,1,w3))

def mlp_fwd_kernel(x_ref,att_ref,pw_ref,pb_ref,gain_ref,shift_ref,w1_ref,b1_ref,w2_ref,b2_ref,
                   resid_ref,act_ref,hid_ref,slope_ref,out_ref,acc_ref):
    j=pl.program_id(1)
    @pl.when(j==0)
    def _():
        g,_,lw=pw_ref.shape
        for b in range(g):
            cols=slice(b*lw,(b+1)*lw)
            part=x_ref[0,:,cols].astype(F32)+pb_ref[:,cols]
            for k in range(g):
                part=part+dot(att_ref[0,:,k*lw:(k+1)*lw],pw_ref[k,cols,:],NN)
            resid_ref[0,:,cols]=part
        resid=resid_ref[0]
        normed,_=normalize(resid)
        act_ref[0]=(normed*gain_ref[...]+shift_ref[...]).astype(BF)
        acc_ref[...]=resid+b2_ref[...]
    pre=dot(act_ref[0],w1_ref[0],NN)+b1_ref[0]
    cdf=0.5+0.5*lax.erf(pre*SQRT_HALF)
    hid=(pre*cdf).astype(BF)
    hid_ref[0]=hid
    slope_ref[0]=(cdf+pre*jnp.exp2(pre*pre*(-0.5*LOG2E))*INV_SQRT_TAU).astype(BF)
    acc_ref[...]+=dot(hid,w2_ref[0],NN)
    @pl.when(j==pl.num_programs(1)-1)
    def _():
        out_ref[0]=acc_ref[...].astype(BF)

def mlp_fwd(at,x,att,pw,pb,gain,shift,w1,b1,w2,b2,tile=1024,n=1,work=1000000):
    _,seq,d=x.shape
    g,_,fw=w1.shape
    ff=g*fw
    tile=min(tile,fw)
    per=fw//tile
    img=pl.BlockSpec((1,seq,d),lambda i,j:(i,0,0))
    own=pl.BlockSpec((1,seq,d),lambda i,j:(at+i,0,0))
    hidden=pl.BlockSpec((1,seq,tile),lambda i,j:(i,0,j))
    return pl.pallas_call(mlp_fwd_kernel,grid=(n,ff//tile),
        in_specs=[own,img,pl.BlockSpec((g,d,d//g),lambda i,j:(0,0,3)),row(d),row(d),row(d),
            pl.BlockSpec((1,d,tile),lambda i,j:(j//per,0,j%per)),pl.BlockSpec((1,1,tile),lambda i,j:(j,0,0)),
            pl.BlockSpec((1,tile,d),lambda i,j:(j//per,j%per,0)),row(d)],
        out_specs=[img,img,hidden,hidden,img],
        out_shape=[jax.ShapeDtypeStruct((n,seq,d),F32),jax.ShapeDtypeStruct((n,seq,d),BF),jax.ShapeDtypeStruct((n,seq,ff),BF),
            jax.ShapeDtypeStruct((n,seq,ff),BF),jax.ShapeDtypeStruct((n,seq,d),BF)],
        scratch_shapes=[pltpu.VMEM((seq,d),F32)],
        **params("mlp_fwd",2*n*seq*d*(d+2*ff),n*seq*(5*d+2*ff)*2+ff*d*4,2*n*seq*ff,work))(x,att,pw,pb,gain,shift,w1,b1.reshape(ff//tile,1,tile),w2,b2)

def mlp_bwd_kernel(cot_ref,slope_ref,w2_ref,w1_ref,resid_ref,gain_ref,pw_ref,
                   dpre_ref,db1_ref,dres_ref,dresb_ref,datt_ref,sums_ref,acc_ref):
    j=pl.program_id(1)
    dpre=dot(cot_ref[0],w2_ref[0],NT)*slope_ref[0].astype(F32)
    db1_ref[0,0]=jnp.sum(dpre,axis=0,keepdims=True)
    dpre_b=dpre.astype(BF)
    dpre_ref[0]=dpre_b
    part=dot(dpre_b,w1_ref[0],NT)
    @pl.when(j==0)
    def _():
        acc_ref[...]=part
    @pl.when(j>0)
    def _():
        acc_ref[...]+=part
    @pl.when(j==pl.num_programs(1)-1)
    def _():
        dact=acc_ref[...]
        normed,inv_std=normalize(resid_ref[0])
        dy=cot_ref[0].astype(F32)
        dres=dy+norm_back(dact*gain_ref[...],normed,inv_std)
        dres_ref[0]=dres
        dresb=dres.astype(BF)
        dresb_ref[0]=dresb
        g,_,lw=pw_ref.shape
        for k in range(g):
            part=0.0
            for b in range(g):
                cols=slice(b*lw,(b+1)*lw)
                part=part+dot(dresb[:,cols],pw_ref[k,cols,:],NT)
            datt_ref[0,:,k*lw:(k+1)*lw]=part.astype(BF)
        sums_ref[0,0:1]=jnp.sum(dact*normed,axis=0,keepdims=True)
        sums_ref[0,1:2]=jnp.sum(dact,axis=0,keepdims=True)
        sums_ref[0,2:3]=jnp.sum(dres,axis=0,keepdims=True)
        sums_ref[0,3:4]=jnp.sum(dy,axis=0,keepdims=True)

def mlp_bwd(at,cot,slope,w2,w1,resid,gain,pw,tile=1024):
    n,seq,d=1,*cot.shape[1:]
    g,_,fw=w1.shape
    ff=g*fw
    tile=min(tile,fw)
    per=fw//tile
    img=pl.BlockSpec((1,seq,d),lambda i,j:(i,0,0))
    own=pl.BlockSpec((1,seq,d),lambda i,j:(at,0,0))
    hidden=pl.BlockSpec((1,seq,tile),lambda i,j:(i,0,j))
    return pl.pallas_call(mlp_bwd_kernel,grid=(n,ff//tile),
        in_specs=[own,hidden,pl.BlockSpec((1,tile,d),lambda i,j:(j//per,j%per,0)),pl.BlockSpec((1,d,tile),lambda i,j:(j//per,0,j%per)),
            img,row(d),pl.BlockSpec((g,d,d//g),lambda i,j:(0,0,3))],
        out_specs=[hidden,pl.BlockSpec((1,1,1,tile),lambda i,j:(i,j,0,0)),img,img,img,pl.BlockSpec((1,4,d),lambda i,j:(i,0,0))],
        out_shape=[jax.ShapeDtypeStruct((n,seq,ff),BF),jax.ShapeDtypeStruct((n,ff//tile,1,tile),F32),jax.ShapeDtypeStruct((n,seq,d),F32),
            jax.ShapeDtypeStruct((n,seq,d),BF),jax.ShapeDtypeStruct((n,seq,d),BF),jax.ShapeDtypeStruct((n,4,d),F32)],
        scratch_shapes=[pltpu.VMEM((seq,d),F32)],
        **params("mlp_bwd",2*n*seq*d*(d+2*ff),n*seq*(6*d+2*ff)*2+ff*d*4))(cot,slope,w2,w1,resid,gain,pw)

def attn_bwd_kernel(qkv_ref,do_ref,w_ref,x_ref,dres_ref,gain_ref,dqkv_ref,qvsum_ref,gt_ref,sums_ref,acc_ref):
    t=pl.program_id(1)
    lw=do_ref.shape[2]
    seq=x_ref.shape[1]
    low=lax.broadcasted_iota(jnp.int32,(seq,PAIR),1)<HD
    for p in range(lw//PAIR):
        at=p*PAIR
        q=qkv_ref[0,:,at:at+PAIR]
        k=qkv_ref[0,:,lw+at:lw+at+PAIR]
        v=qkv_ref[0,:,2*lw+at:2*lw+at+PAIR]
        do=do_ref[0,:,at:at+PAIR]
        dqs=[];dks=[];dvs=[]
        for sel in (low,~low):
            km=jnp.where(sel,k,jnp.zeros_like(k))
            vm=jnp.where(sel,v,jnp.zeros_like(v))
            st=dot(km,q,NT)*(HD**-0.5*LOG2E)
            e=jnp.exp2(st-jnp.max(st,axis=0,keepdims=True))
            pt=e*(1.0/jnp.sum(e,axis=0,keepdims=True))
            dp=dot(vm,do,NT)
            delta=jnp.sum(pt*dp,axis=0,keepdims=True)
            ds=(pt*((dp-delta)*HD**-0.5)).astype(BF)
            dvs.append(dot(pt.astype(BF),do,NN))
            dks.append(dot(ds,q,NN))
            dqs.append(dot(ds,k,TN))
        dq=jnp.where(low,dqs[0],dqs[1]); dk=jnp.where(low,dks[0],dks[1]); dv=jnp.where(low,dvs[0],dvs[1])
        dqkv_ref[0,:,at:at+PAIR]=dq.astype(BF)
        dqkv_ref[0,:,lw+at:lw+at+PAIR]=dk.astype(BF)
        dqkv_ref[0,:,2*lw+at:2*lw+at+PAIR]=dv.astype(BF)
        qvsum_ref[0,0,0:1,at:at+PAIR]=jnp.sum(dq,axis=0,keepdims=True)
        qvsum_ref[0,0,1:2,at:at+PAIR]=jnp.sum(dv,axis=0,keepdims=True)
    part=dot(dqkv_ref[0],w_ref[0],NT)
    @pl.when(t==0)
    def _():
        acc_ref[...]=part
    @pl.when(t>0)
    def _():
        acc_ref[...]+=part
    @pl.when(t==pl.num_programs(1)-1)
    def _():
        dact=acc_ref[...]
        normed,inv_std=normalize(x_ref[0].astype(F32))
        gt_ref[0]=(dres_ref[0]+norm_back(dact*gain_ref[...],normed,inv_std)).astype(BF)
        sums_ref[0,0:1]=jnp.sum(dact*normed,axis=0,keepdims=True)
        sums_ref[0,1:2]=jnp.sum(dact,axis=0,keepdims=True)

def attn_bwd(at,qkv,do,w,x,dres,gain):
    n,seq,d=1,*x.shape[1:]
    g=w.shape[0]
    w3=qkv.shape[2]//g
    lw=w3//3
    img=pl.BlockSpec((1,seq,d),lambda i,t:(i,0,0))
    return pl.pallas_call(attn_bwd_kernel,grid=(n,g),
        in_specs=[pl.BlockSpec((1,seq,w3),lambda i,t:(i,0,t)),pl.BlockSpec((1,seq,lw),lambda i,t:(i,0,t)),
            pl.BlockSpec((1,d,w3),lambda i,t:(t,0,0)),pl.BlockSpec((1,seq,d),lambda i,t:(at,0,0)),img,row(d)],
        out_specs=[pl.BlockSpec((1,seq,w3),lambda i,t:(i,0,t)),pl.BlockSpec((1,1,2,lw),lambda i,t:(i,t,0,0)),img,pl.BlockSpec((1,2,d),lambda i,t:(i,0,0))],
        out_shape=[jax.ShapeDtypeStruct((n,seq,g*w3),BF),jax.ShapeDtypeStruct((n,g,2,lw),F32),jax.ShapeDtypeStruct((n,seq,d),BF),jax.ShapeDtypeStruct((n,2,d),F32)],
        scratch_shapes=[pltpu.VMEM((seq,d),F32)],
        **params("attn_bwd",2*n*seq*d*g*w3+40*n*seq*seq*g*lw,n*seq*(2*g*w3+g*lw+4*d)*2+g*w3*d*2,n*g*lw//HD*seq*seq))(qkv,do,w,x,dres,gain)


def cut(total,out_ref):
    out_ref[...]=total.astype(BF).reshape(out_ref.shape)

def image_sum(refs):
    n=len(refs)//2
    return sum(dot(l[0],r[0],TN) for l,r in zip(refs[:n],refs[n:]))

def grad_kernel(*refs):
    cut(image_sum(refs[:-1]),refs[-1])

def grad_fc1_kernel(*refs):
    out_ref=refs[-1]
    half=len(refs)//2
    n_dp,_,rows,width=out_ref.shape
    fw=refs[half-1].shape[2]
    lw=width-fw
    out_ref[:,0,:,:fw]=image_sum(refs[:half]).astype(BF).reshape(n_dp,rows,fw)
    proj=image_sum(refs[half:-1]).astype(BF)
    per=lw//rows
    for b in range(n_dp//per):
        out_ref[b*per:(b+1)*per,0,:,fw:]=proj[:,b*lw:(b+1)*lw].reshape(per,rows,lw)

def shard_grads(kernel,name,n_dp,g,rows,width,specs,ops):
    return pl.pallas_call(kernel,
        grid=(g,),in_specs=specs,out_specs=pl.BlockSpec((n_dp,1,rows//n_dp,width),lambda k:(0,k,0,0)),
        out_shape=jax.ShapeDtypeStruct((n_dp,g,rows//n_dp,width),BF),
        **params(name,0,0))(*ops)

def whole(ops): return [pl.BlockSpec((1,*a.shape[1:]),lambda k:(0,0,0)) for a in ops]

def both(a): return [pl.BlockSpec((1,*a.shape[1:]),lambda k,i=i:(i,0,0)) for i in range(a.shape[0])]

def part(ops,g): return [pl.BlockSpec((1,a.shape[1],a.shape[2]//g),lambda k:(0,0,k)) for a in ops]

def grad_fc2(hid,cot,n_dp,g):
    ff,d=hid[0].shape[2],cot.shape[2]
    return shard_grads(grad_kernel,"grad_fc2",n_dp,g,ff//g,d,part(hid,g)+both(cot),(*hid,*[cot]*len(hid)))

def grad_fc1(act,dpre,att,dres,n_dp,g):
    ff,d=dpre[0].shape[2],act[0].shape[2]
    return shard_grads(grad_fc1_kernel,"grad_fc1",n_dp,g,d,ff//g+d//g,
        whole(act)+part(dpre,g)+part(att,g)+whole(dres),(*act,*dpre,*att,*dres))

def grad_qkv(act,dqkv,n_dp,g):
    w,d=dqkv[0].shape[2],act[0].shape[2]
    return shard_grads(grad_kernel,"grad_qkv",n_dp,g,d,w//g,whole(act)+part(dqkv,g),(*act,*dqkv))

def interleave(rows,out_ref):
    out_ref[...]=jnp.swapaxes(jnp.stack([r.astype(F32) for r in rows],axis=0),0,1).astype(BF)

def weave_kernel(*refs):
    interleave([ref[t] for t in range(refs[0].shape[0]) for ref in refs[:-1]],refs[-1])

def weave(parts,tile=64):
    n_t,seq,d=parts[0].shape
    n=n_t*len(parts)
    out=pl.pallas_call(weave_kernel,grid=(pl.cdiv(seq,tile),),
        in_specs=[pl.BlockSpec((n_t,tile,d),lambda r:(0,r,0))]*len(parts),
        out_specs=pl.BlockSpec((tile,n,d),lambda r:(r,0,0)),
        out_shape=jax.ShapeDtypeStruct((seq,n,d),BF),**params("weave",0,0))(*parts)
    return out.transpose(1,0,2)

def adamw(weight_old, moment_one, moment_two, grad_sum, rate_value, decay_value):
    new_one = BETA_ONE * moment_one + (1.0 - BETA_ONE) * grad_sum
    new_two = BETA_TWO * moment_two + (1.0 - BETA_TWO) * grad_sum * grad_sum
    one_hat = new_one / (1.0 - BETA_ONE**STEP)
    two_hat = new_two / (1.0 - BETA_TWO**STEP)
    new_weight = weight_old - rate_value * (
        one_hat / (jnp.sqrt(two_hat) + ADAM_EPS) + decay_value * weight_old
    )
    return (new_weight, new_one, new_two)


def shift(value, axis, by):
    n = lax.axis_size(axis)
    return lax.ppermute(value, axis, [(i, (i + by) % n) for i in range(n)])


def swap(value, axis, mask):
    n = lax.axis_size(axis)
    return lax.ppermute(value, axis, [(i, i ^ mask) for i in range(n)])


def spread_moves(bufs, c, p, units, target):
    half = units * p // 2
    moves = []
    for flip, buf in enumerate(bufs):
        base = c ^ flip
        for at, slot in enumerate((base, base ^ 2, base ^ 4)):
            first = pl.multiple_of(slot * p, p)
            moves += [(buf.at[pl.ds((at * units + k) * p, p)], target(k, first, p)) for k in range(units)]
        first = pl.multiple_of((base ^ 6) * p, p)
        moves += [(buf.at[pl.ds((3 * units + k) * p, p)], target(k, first, p)) for k in range(units)]
    return moves


def run_copies(moves, sems):
    copies = [pltpu.make_async_copy(src, dst, sems.at[i]) for i, (src, dst) in enumerate(moves)]
    for copy in copies:
        copy.start()
    for copy in copies:
        copy.wait()


def place_kernel(at_ref, own_ref, near_ref, far_ref, out_ref, sems):
    p = near_ref.shape[0] // 12
    moves = spread_moves((near_ref, far_ref), at_ref[0], p, 3, lambda k, first, n: out_ref.at[k + 1, pl.ds(first, n)])
    run_copies([(own_ref, out_ref.at[0])] + moves, sems)


def spread_kernel(at_ref, near_ref, far_ref, out_ref, sems):
    p = near_ref.shape[0] // 4
    run_copies(spread_moves((near_ref, far_ref), at_ref[0], p, 1, lambda k, first, n: out_ref.at[pl.ds(first, n)]), sems)


def dma_call(kernel, name, n, out_shape, ops):
    at = lax.axis_index("dp").reshape(1).astype(jnp.int32)
    return pl.pallas_call(
        kernel,
        in_specs=[pl.BlockSpec(memory_space=pltpu.SMEM)] + [pl.BlockSpec(memory_space=pltpu.VMEM)] * len(ops),
        out_specs=pl.BlockSpec(memory_space=pl.ANY),
        out_shape=out_shape,
        scratch_shapes=[pltpu.SemaphoreType.DMA((n,))],
        **params(name, 0, 0),
    )(at, *ops)


def after(value, *earlier):
    return lax.optimization_barrier((value, *earlier))[0]


def tie(*values):
    return lax.optimization_barrier(values)


def shards(piece):
    return [shift(piece, "tensor", k) for k in range(1, lax.axis_size("tensor"))]


def fetch(mine):
    if lax.axis_size("dp") != 8:
        return mine, mine
    return swap(mine, "dp", 2), swap(mine, "dp", 4)


def fetch_diagonal(xs, ys):
    half = xs.shape[0] // 2
    if lax.axis_size("dp") != 8:
        return xs[:half], ys[half:]
    return swap(xs[:half], "dp", 4), swap(ys[half:], "dp", 2)


def finish(own, mine, xs, ys, da, db, name):
    if lax.axis_size("dp") != 8:
        every = lax.all_gather(mine.reshape(lax.axis_size("tensor") - 1, -1, own.shape[1]), "dp", axis=1, tiled=True)
        return jnp.concatenate([own[None], every], 0)
    near = jnp.concatenate([mine, xs, ys, da, db], 0)
    shape = jax.ShapeDtypeStruct((4, *own.shape), own.dtype)
    return dma_call(place_kernel, name, 25, shape, (own, near, swap(near, "dp", 1)))


def reduce_dp(parts):
    return lax.psum_scatter(parts, "dp", scatter_dimension=0, tiled=False)


def parts_of(value):
    parts = []
    for _ in range(3):
        parts.append(lax.reduce_precision(value, 8, 7))
        value = value - parts[-1]
    return [v.astype(BF) for v in parts]


def sum_chain(value):
    for axis in ("dp", "tensor"):
        mask = 1
        while mask < lax.axis_size(axis):
            value = value + (yield swap(value, axis, mask))
            mask *= 2
    return value


def reduce_chain(part, name):
    n_t = part.shape[0]
    up, down = part[1], part[n_t - 1]
    for step in range(1, n_t):
        up, down = yield (
            lax.ppermute(up, "tensor", [(i, i + 1) for i in range(step)]),
            lax.ppermute(down, "tensor", [(n_t - 1 - i, n_t - 2 - i) for i in range(step)]),
        )
        if step < n_t - 1:
            up = (up.astype(F32) + part[step + 1].astype(F32)).astype(BF)
            down = (down.astype(F32) + part[n_t - 1 - step].astype(F32)).astype(BF)
    mine = (part[0].astype(F32) + up.astype(F32) + down.astype(F32)).astype(BF)
    if lax.axis_size("dp") != 8:
        return lax.all_gather(mine, "dp", axis=0, tiled=True).astype(F32)
    xs, ys = yield fetch(mine)
    da, db = yield fetch_diagonal(xs, ys)
    near = jnp.concatenate([mine, xs, ys, da, db], 0)
    far = yield swap(near, "dp", 1)
    shape = jax.ShapeDtypeStruct((8 * mine.shape[0], mine.shape[1]), mine.dtype)
    return dma_call(spread_kernel, name, 8, shape, (near, far)).astype(F32)


def run_chains(chains, work, made):
    live, results, step = {}, [None] * len(chains), 0
    while step == 0 or live or work or any(begin >= step for begin, _ in chains):
        moved = {}
        for at, (begin, make) in enumerate(chains):
            if begin == step:
                live[at] = make()
                moved[at] = next(live[at])
            elif at in live:
                try:
                    moved[at] = live[at].send(kept[at])
                except StopIteration as end:
                    results[at] = end.value
                    del live[at]
        if work:
            made.append(work.pop(0)(made, results))
            moved, made[-1] = tie(moved, made[-1])
        else:
            moved = tie(moved)[0]
        kept = moved
        step += 1
    return results


def per_device(*args):
    tokens, cotangent = args[0], args[1]
    weights, firsts, seconds = args[2:10], args[10:18], args[18:26]
    qkv_weight, qv_bias, proj_weight, fc1_weight, fc1_bias, fc2_weight, norm_gains, shift_biases = weights
    n_t = lax.axis_size("tensor")
    n_dp = lax.axis_size("dp")
    t_at = lax.axis_index("tensor")
    dp_at = lax.axis_index("dp")
    width = tokens.shape[2]
    own = tokens.shape[0] // n_t
    lw = qkv_weight.shape[2]
    fw = fc1_weight.shape[1]

    def proj_pack(value):
        return value.reshape(lw, n_t, lw).transpose(1, 0, 2).reshape(width, lw)

    def proj_unpack(value):
        return value.reshape(n_t, lw, lw).transpose(1, 0, 2).reshape(lw, width)

    mix = jnp.concatenate([qkv_weight[:, 0], qkv_weight[:, 1], qkv_weight[:, 2], proj_pack(proj_weight)], axis=1)
    p = width // n_dp
    mix = mix.astype(BF)
    biases = jnp.concatenate([qv_bias.reshape(-1), fc1_bias])
    flat = jnp.concatenate(parts_of(biases))
    columns = mix.shape[1]
    extra = 16 * pl.cdiv(flat.size, 16 * columns)
    flat = jnp.pad(flat, (0, extra * columns - flat.size)).reshape(extra, columns)

    def dp_rows(w):
        return lax.dynamic_slice_in_dim(w, dp_at * (w.shape[0] // n_dp), w.shape[0] // n_dp, 0).astype(BF)

    p0, p1, p2 = dp_rows(mix), dp_rows(fc1_weight), dp_rows(fc2_weight)
    z0 = shards(jnp.concatenate([p0, flat], axis=0))
    x = lax.dynamic_slice_in_dim(tokens, t_at * own, own, 0)
    cot = lax.dynamic_slice_in_dim(cotangent, t_at * own, own, 0)
    fc1, fc2 = fc1_weight.astype(BF), fc2_weight.astype(BF)
    z0, x, cot, fc1, fc2, p1, p2 = tie(z0, x, cot, fc1, fc2, p1, p2)
    mine0 = jnp.concatenate([z[:p] for z in z0], 0)
    near0, z1 = fetch(mine0), shards(p1)
    near0, z1, p2 = tie(near0, z1, p2)
    mine1 = jnp.concatenate(z1, 0)
    diag0, near1, z2 = fetch_diagonal(*near0), fetch(mine1), shards(p2)
    diag0, near1, z2 = tie(diag0, near1, z2)
    mine2 = jnp.concatenate(z2, 0)
    w_mix = finish(mix, mine0, *near0, *diag0, name="place_mix")
    diag1, near2 = fetch_diagonal(*near1), fetch(mine2)
    flat = jnp.stack([z[p:].reshape(-1)[: 3 * biases.size].astype(F32).reshape(3, -1) for z in z0])
    bias_rel = jnp.concatenate([biases[None], flat[:, 0] + flat[:, 1] + flat[:, 2]], axis=0)
    qv_rel = bias_rel[:, : 2 * lw].reshape(n_t, 2, lw)
    qkv_bias = jnp.stack([qv_rel[:, 0], jnp.zeros_like(qv_rel[:, 0]), qv_rel[:, 1]], axis=1).reshape(n_t, 3 * lw)
    b1_rel = bias_rel[:, 2 * lw :].reshape(-1)
    gain1, gain2 = norm_gains[0:1], norm_gains[1:2]

    def gather(mine):
        return lax.all_gather(mine[0], "tensor", axis=0, tiled=False)

    act1, qkv, attended = [], [], []
    resid, act2, hidden, slope, out_all = [], [], [], [], []
    for i in range(own):
        made = qkv_attn(i, after(x, *hidden[-1:]), gain1, shift_biases[0:1], w_mix, qkv_bias)
        for kept, value in zip((act1, qkv, attended), made):
            kept.append(value)
        if i == 0:
            diag1, near2, head = tie(diag1, near2, attended[0])
            diag2 = fetch_diagonal(*near2)
            w_fc1 = finish(after(fc1, head), mine1, *near1, *diag1, name="place_fc1")
            w_fc1, diag2 = tie(w_fc1, diag2)
            w_fc2 = finish(fc2, mine2, *near2, *diag2, name="place_fc2")
        *kept, out_own = mlp_fwd(
            i, x, attended[i], w_mix, shift_biases[2:3], gain2, shift_biases[1:2], w_fc1, b1_rel, w_fc2, shift_biases[3:4]
        )
        for made, value in zip((resid, act2, hidden, slope), kept):
            made.append(value)
        out_all.append(gather(out_own))
    g_fc2 = grad_fc2(hidden, cot, n_dp, n_t)
    slope[0] = after(slope[0], g_fc2)
    part_fc2 = reduce_dp(g_fc2)
    d_pre, g_b1, d_resid, d_resid_b, d_att, sums2 = [], [], [], [], [], []
    for i in range(own):
        made = mlp_bwd(i, cot, after(slope[i], *d_pre[-1:]), w_fc2, w_fc1, resid[i], gain2, w_mix)
        for kept, value in zip((d_pre, g_b1, d_resid, d_resid_b, d_att, sums2), made):
            kept.append(value)
    part_fc1 = grad_fc1(act2, d_pre, attended, d_resid_b, n_dp, n_t)
    part_fc1, *d_att = tie(part_fc1, *d_att)
    part_fc1 = reduce_dp(part_fc1)
    d_att[0], out_all[0], part_fc2 = tie(d_att[0], out_all[0], part_fc2)
    gt_all = [None] * own

    def attention_back(i):
        def run(made, results):
            d = after(d_att[i], *(made[-1] if made else ()))
            dq, gq, gt_own, s1 = attn_bwd(i, qkv[i], d, w_mix, x, d_resid[i], gain1)
            gt_all[i] = gather(gt_own)
            return dq, gq, s1

        return run

    def attention_grad(made, results):
        d_qkv = [m[0] for m in made]
        d_qkv[-1], out_all[-1] = tie(d_qkv[-1], out_all[-1])
        return grad_qkv(act1, d_qkv, n_dp, n_t)

    rates = (
        1.2 / math.sqrt(D),
        0.6,
        0.6 / math.sqrt(max(D // 128, 1)),
        0.6 / math.sqrt(D),
        0.3,
        0.6 / math.sqrt(max(FF // 8, 1)),
        3.0,
        3.0,
    )
    decays = (MATRIX_DECAY, 0.0, MATRIX_DECAY, MATRIX_DECAY, 0.0, MATRIX_DECAY, 0.0, 0.0)

    def step(at, grad):
        return adamw(weights[at], firsts[at], seconds[at], grad, rates[at], decays[at])

    order = (t_at + n_t - jnp.arange(n_t)) % n_t

    def vectors():
        _, g_qv, sums1 = (sum(v[1:], v[0]) for v in zip(*made[:own]))
        rel = jnp.concatenate([g_qv.reshape(n_t, -1), sum(g_b1).reshape(n_t, -1)], axis=1)
        rel = jnp.take(rel, order, axis=0)
        return jnp.concatenate([rel.reshape(-1), sums1.reshape(-1), sum(sums2).reshape(-1)])

    def fc2_step(made, results):
        return results[1], step(5, results[1])

    def fc1_step(made, results):
        g_fc1, g_proj = results[2][:, :fw], proj_unpack(results[2][:, fw:])
        return g_fc1, g_proj, step(3, g_fc1), step(2, g_proj)

    def waits_for(i):
        return lambda made, results: gt_all[i]

    def nothing(made, results):
        return ()

    made = []
    chains = [
        (own + 1, lambda: sum_chain(vectors())),
        (0, lambda: reduce_chain(part_fc2, "spread_fc2")),
        (own + 1, lambda: reduce_chain(part_fc1, "spread_fc1")),
        (own + 4, lambda: reduce_chain(reduce_dp(made[own]), "spread_qkv")),
    ]
    work = [attention_back(i) for i in range(own)] + [
        attention_grad,
        lambda made, results: weave(out_all),
        waits_for(0),
        nothing,
        nothing if n_t > 4 else fc2_step,
        nothing,
        nothing,
        nothing if n_t > 4 else fc1_step,
        waits_for(-1),
    ]
    flat, g_fc2, g_fc1, g_qkv = run_chains(chains, work, made)
    output, gt_all[0], gt_all[-1] = made[own + 1], made[own + 2], made[-1]
    if n_t > 4:
        made[own + 4], made[own + 7] = fc2_step(made, (None, g_fc2)), fc1_step(made, (None, None, g_fc1))
    (g_fc2, new_fc2), (g_fc1, g_proj, new_fc1, new_proj) = made[own + 4], made[own + 7]
    rel = 2 * lw + fw
    g_qkv = jnp.stack([g_qkv[:, i * lw : (i + 1) * lw] for i in range(3)], axis=1)
    mine = lax.dynamic_index_in_dim(flat[: n_t * rel].reshape(n_t, rel), t_at, 0, keepdims=False)
    rest = flat[n_t * rel :].reshape(6, width)
    g_gains = jnp.stack([rest[0], rest[2]])
    g_shifts = jnp.stack([rest[1], rest[3], rest[4], rest[5]])
    grads = (g_qkv, mine[: 2 * lw].reshape(2, lw), g_proj, g_fc1, mine[2 * lw :], g_fc2, g_gains, g_shifts)
    updated = [step(at, grad) for at, grad in enumerate(grads)]
    updated[3], updated[5], updated[2] = new_fc1, new_fc2, new_proj
    gt_all[-1], *_ = tie(gt_all[-1], *(u[0] for u in updated))
    grad_tokens = weave(gt_all)
    return (
        output,
        grad_tokens,
        *grads,
        *(u[0] for u in updated),
        *(u[1] for u in updated),
        *(u[2] for u in updated),
    )


def solution(mesh):
    weights = (
        P(None, None, "tensor"),
        P(None, "tensor"),
        P("tensor", None),
        P(None, "tensor"),
        P("tensor"),
        P("tensor", None),
        P(),
        P(),
    )
    images = (P("dp", None, None), P("dp", None, None))
    return jax.shard_map(
        per_device,
        mesh=mesh,
        in_specs=images + weights * 3,
        out_specs=images + weights * 4,
        check_vma=False,
    )
```

```python
import math

import jax
import jax.numpy as jnp
from jax import lax
from jax.experimental import pallas as pl
from jax.experimental.pallas import tpu as pltpu
from jax.sharding import PartitionSpec as P

D = 1024
FF = 4096
STEP = 3
BETA_ONE = 0.9
BETA_TWO = 0.999
ADAM_EPS = 1e-08
MATRIX_DECAY = 0.05

HD=64
LOG2E=1.4426950408889634
NORM_EPS = 1e-05
SQRT_HALF = 0.7071067811865476
INV_SQRT_TAU = 0.3989422804014327
NT=(((1,),(1,)),((),()))
NN=(((1,),(0,)),((),()))
TN=(((0,),(0,)),((),()))
BF=jnp.bfloat16
F32=jnp.float32
VLIM=36*2**20
PAIR=2*HD

def dot(a,b,dims):
    return lax.dot_general(a,b,dims,preferred_element_type=jnp.float32)

def normalize(v):
    center=v-jnp.mean(v,axis=-1,keepdims=True)
    inv_std=lax.rsqrt(jnp.mean(center*center,axis=-1,keepdims=True)+NORM_EPS)
    return center*inv_std,inv_std

def norm_back(d_normed,normed,inv_std):
    return inv_std*(d_normed-jnp.mean(d_normed,axis=-1,keepdims=True)-normed*jnp.mean(d_normed*normed,axis=-1,keepdims=True))

def qkv_attn_kernel(x_ref,gain_ref,shift_ref,w_ref,b_ref,act_ref,qkv_ref,out_ref):
    t=pl.program_id(1)
    @pl.when(t==0)
    def _():
        normed,_=normalize(x_ref[0].astype(F32))
        act_ref[0]=(normed*gain_ref[...]+shift_ref[...]).astype(BF)
    qkv_ref[0]=(dot(act_ref[0],w_ref[0],NN)+b_ref[0]).astype(BF)
    lw=out_ref.shape[2]
    seq=x_ref.shape[1]
    low=lax.broadcasted_iota(jnp.int32,(seq,PAIR),1)<HD
    for p in range(lw//PAIR):
        at=p*PAIR
        q=qkv_ref[0,:,at:at+PAIR]
        k=qkv_ref[0,:,lw+at:lw+at+PAIR]
        v=qkv_ref[0,:,2*lw+at:2*lw+at+PAIR]
        outs=[]
        for sel in (low,~low):
            s=dot(jnp.where(sel,q,jnp.zeros_like(q)),k,NT)*(HD**-0.5*LOG2E)
            e=jnp.exp2(s-jnp.max(s,axis=1,keepdims=True))
            l=jnp.sum(e,axis=1,keepdims=True)
            outs.append(dot(e.astype(BF),v,NN)/l)
        out_ref[0,:,at:at+PAIR]=jnp.where(low,outs[0],outs[1]).astype(BF)

def params(name,flops,nbytes,trans=0,work=1000000,limit=VLIM):
    return dict(name=name,compiler_params=pltpu.CompilerParams(vmem_limit_bytes=limit),
        cost_estimate=pl.CostEstimate(flops=int(work),bytes_accessed=1000000,transcendentals=0))

def row(width): return pl.BlockSpec((1,width),lambda *_:(0,0))

def qkv_attn(at,x,gain,shift,w,b,n=1,work=1000000):
    _,seq,d=x.shape
    g=w.shape[0]
    w3=b.shape[1]
    lw=w3//3
    return pl.pallas_call(qkv_attn_kernel,grid=(n,g),
        in_specs=[pl.BlockSpec((1,seq,d),lambda i,t:(at+i,0,0)),row(d),row(d),
            pl.BlockSpec((1,d,w3),lambda i,t:(t,0,0)),pl.BlockSpec((1,1,w3),lambda i,t:(t,0,0))],
        out_specs=[pl.BlockSpec((1,seq,d),lambda i,t:(i,0,0)),pl.BlockSpec((1,seq,w3),lambda i,t:(i,0,t)),pl.BlockSpec((1,seq,lw),lambda i,t:(i,0,t))],
        out_shape=[jax.ShapeDtypeStruct((n,seq,d),BF),jax.ShapeDtypeStruct((n,seq,g*w3),BF),jax.ShapeDtypeStruct((n,seq,g*lw),BF)],
        **params("qkv_attn",2*n*seq*d*g*w3+16*n*seq*seq*g*lw,n*seq*(2*d+g*w3+g*lw)*2,n*g*lw//HD*seq*seq,work))(x,gain,shift,w,b.reshape(g,1,w3))

def mlp_fwd_kernel(x_ref,att_ref,pw_ref,pb_ref,gain_ref,shift_ref,w1_ref,b1_ref,w2_ref,b2_ref,
                   resid_ref,act_ref,hid_ref,slope_ref,out_ref,acc_ref):
    j=pl.program_id(1)
    @pl.when(j==0)
    def _():
        g,_,lw=pw_ref.shape
        for b in range(g):
            cols=slice(b*lw,(b+1)*lw)
            part=x_ref[0,:,cols].astype(F32)+pb_ref[:,cols]
            for k in range(g):
                part=part+dot(att_ref[0,:,k*lw:(k+1)*lw],pw_ref[k,cols,:],NN)
            resid_ref[0,:,cols]=part
        resid=resid_ref[0]
        normed,_=normalize(resid)
        act_ref[0]=(normed*gain_ref[...]+shift_ref[...]).astype(BF)
        acc_ref[...]=resid+b2_ref[...]
    pre=dot(act_ref[0],w1_ref[0],NN)+b1_ref[0]
    cdf=0.5+0.5*lax.erf(pre*SQRT_HALF)
    hid=(pre*cdf).astype(BF)
    hid_ref[0]=hid
    slope_ref[0]=(cdf+pre*jnp.exp2(pre*pre*(-0.5*LOG2E))*INV_SQRT_TAU).astype(BF)
    acc_ref[...]+=dot(hid,w2_ref[0],NN)
    @pl.when(j==pl.num_programs(1)-1)
    def _():
        out_ref[0]=acc_ref[...].astype(BF)

def mlp_fwd(at,x,att,pw,pb,gain,shift,w1,b1,w2,b2,tile=1024,n=1,work=1000000):
    _,seq,d=x.shape
    g,_,fw=w1.shape
    ff=g*fw
    tile=min(tile,fw)
    per=fw//tile
    img=pl.BlockSpec((1,seq,d),lambda i,j:(i,0,0))
    own=pl.BlockSpec((1,seq,d),lambda i,j:(at+i,0,0))
    hidden=pl.BlockSpec((1,seq,tile),lambda i,j:(i,0,j))
    return pl.pallas_call(mlp_fwd_kernel,grid=(n,ff//tile),
        in_specs=[own,img,pl.BlockSpec((g,d,d//g),lambda i,j:(0,0,3)),row(d),row(d),row(d),
            pl.BlockSpec((1,d,tile),lambda i,j:(j//per,0,j%per)),pl.BlockSpec((1,1,tile),lambda i,j:(j,0,0)),
            pl.BlockSpec((1,tile,d),lambda i,j:(j//per,j%per,0)),row(d)],
        out_specs=[img,img,hidden,hidden,img],
        out_shape=[jax.ShapeDtypeStruct((n,seq,d),F32),jax.ShapeDtypeStruct((n,seq,d),BF),jax.ShapeDtypeStruct((n,seq,ff),BF),
            jax.ShapeDtypeStruct((n,seq,ff),BF),jax.ShapeDtypeStruct((n,seq,d),BF)],
        scratch_shapes=[pltpu.VMEM((seq,d),F32)],
        **params("mlp_fwd",2*n*seq*d*(d+2*ff),n*seq*(5*d+2*ff)*2+ff*d*4,2*n*seq*ff,work,52*2**20))(x,att,pw,pb,gain,shift,w1,b1.reshape(ff//tile,1,tile),w2,b2)

def mlp_bwd_kernel(cot_ref,slope_ref,w2_ref,w1_ref,resid_ref,gain_ref,pw_ref,
                   dpre_ref,db1_ref,dres_ref,dresb_ref,datt_ref,sums_ref,acc_ref):
    j=pl.program_id(1)
    dpre=dot(cot_ref[0],w2_ref[0],NT)*slope_ref[0].astype(F32)
    db1_ref[0,0]=jnp.sum(dpre,axis=0,keepdims=True)
    dpre_b=dpre.astype(BF)
    dpre_ref[0]=dpre_b
    part=dot(dpre_b,w1_ref[0],NT)
    @pl.when(j==0)
    def _():
        acc_ref[...]=part
    @pl.when(j>0)
    def _():
        acc_ref[...]+=part
    @pl.when(j==pl.num_programs(1)-1)
    def _():
        dact=acc_ref[...]
        normed,inv_std=normalize(resid_ref[0])
        dy=cot_ref[0].astype(F32)
        dres=dy+norm_back(dact*gain_ref[...],normed,inv_std)
        dres_ref[0]=dres
        dresb=dres.astype(BF)
        dresb_ref[0]=dresb
        g,_,lw=pw_ref.shape
        for k in range(g):
            part=0.0
            for b in range(g):
                cols=slice(b*lw,(b+1)*lw)
                part=part+dot(dresb[:,cols],pw_ref[k,cols,:],NT)
            datt_ref[0,:,k*lw:(k+1)*lw]=part.astype(BF)
        sums_ref[0,0:1]=jnp.sum(dact*normed,axis=0,keepdims=True)
        sums_ref[0,1:2]=jnp.sum(dact,axis=0,keepdims=True)
        sums_ref[0,2:3]=jnp.sum(dres,axis=0,keepdims=True)
        sums_ref[0,3:4]=jnp.sum(dy,axis=0,keepdims=True)

def mlp_bwd(at,cot,slope,w2,w1,resid,gain,pw,tile=1024):
    n,seq,d=1,*cot.shape[1:]
    g,_,fw=w1.shape
    ff=g*fw
    tile=min(tile,fw)
    per=fw//tile
    img=pl.BlockSpec((1,seq,d),lambda i,j:(i,0,0))
    own=pl.BlockSpec((1,seq,d),lambda i,j:(at,0,0))
    hidden=pl.BlockSpec((1,seq,tile),lambda i,j:(i,0,j))
    return pl.pallas_call(mlp_bwd_kernel,grid=(n,ff//tile),
        in_specs=[own,hidden,pl.BlockSpec((1,tile,d),lambda i,j:(j//per,j%per,0)),pl.BlockSpec((1,d,tile),lambda i,j:(j//per,0,j%per)),
            img,row(d),pl.BlockSpec((g,d,d//g),lambda i,j:(0,0,3))],
        out_specs=[hidden,pl.BlockSpec((1,1,1,tile),lambda i,j:(i,j,0,0)),img,img,img,pl.BlockSpec((1,4,d),lambda i,j:(i,0,0))],
        out_shape=[jax.ShapeDtypeStruct((n,seq,ff),BF),jax.ShapeDtypeStruct((n,ff//tile,1,tile),F32),jax.ShapeDtypeStruct((n,seq,d),F32),
            jax.ShapeDtypeStruct((n,seq,d),BF),jax.ShapeDtypeStruct((n,seq,d),BF),jax.ShapeDtypeStruct((n,4,d),F32)],
        scratch_shapes=[pltpu.VMEM((seq,d),F32)],
        **params("mlp_bwd",2*n*seq*d*(d+2*ff),n*seq*(6*d+2*ff)*2+ff*d*4))(cot,slope,w2,w1,resid,gain,pw)

def attn_bwd_kernel(qkv_ref,do_ref,w_ref,x_ref,dres_ref,gain_ref,dqkv_ref,qvsum_ref,gt_ref,sums_ref,acc_ref):
    t=pl.program_id(1)
    lw=do_ref.shape[2]
    seq=x_ref.shape[1]
    low=lax.broadcasted_iota(jnp.int32,(seq,PAIR),1)<HD
    for p in range(lw//PAIR):
        at=p*PAIR
        q=qkv_ref[0,:,at:at+PAIR]
        k=qkv_ref[0,:,lw+at:lw+at+PAIR]
        v=qkv_ref[0,:,2*lw+at:2*lw+at+PAIR]
        do=do_ref[0,:,at:at+PAIR]
        dqs=[];dks=[];dvs=[]
        for sel in (low,~low):
            km=jnp.where(sel,k,jnp.zeros_like(k))
            vm=jnp.where(sel,v,jnp.zeros_like(v))
            st=dot(km,q,NT)*(HD**-0.5*LOG2E)
            e=jnp.exp2(st-jnp.max(st,axis=0,keepdims=True))
            pt=e*(1.0/jnp.sum(e,axis=0,keepdims=True))
            dp=dot(vm,do,NT)
            delta=jnp.sum(pt*dp,axis=0,keepdims=True)
            ds=(pt*((dp-delta)*HD**-0.5)).astype(BF)
            dvs.append(dot(pt.astype(BF),do,NN))
            dks.append(dot(ds,q,NN))
            dqs.append(dot(ds,k,TN))
        dq=jnp.where(low,dqs[0],dqs[1]); dk=jnp.where(low,dks[0],dks[1]); dv=jnp.where(low,dvs[0],dvs[1])
        dqkv_ref[0,:,at:at+PAIR]=dq.astype(BF)
        dqkv_ref[0,:,lw+at:lw+at+PAIR]=dk.astype(BF)
        dqkv_ref[0,:,2*lw+at:2*lw+at+PAIR]=dv.astype(BF)
        qvsum_ref[0,0,0:1,at:at+PAIR]=jnp.sum(dq,axis=0,keepdims=True)
        qvsum_ref[0,0,1:2,at:at+PAIR]=jnp.sum(dv,axis=0,keepdims=True)
    part=dot(dqkv_ref[0],w_ref[0],NT)
    @pl.when(t==0)
    def _():
        acc_ref[...]=part
    @pl.when(t>0)
    def _():
        acc_ref[...]+=part
    @pl.when(t==pl.num_programs(1)-1)
    def _():
        dact=acc_ref[...]
        normed,inv_std=normalize(x_ref[0].astype(F32))
        gt_ref[0]=(dres_ref[0]+norm_back(dact*gain_ref[...],normed,inv_std)).astype(BF)
        sums_ref[0,0:1]=jnp.sum(dact*normed,axis=0,keepdims=True)
        sums_ref[0,1:2]=jnp.sum(dact,axis=0,keepdims=True)

def attn_bwd(at,qkv,do,w,x,dres,gain):
    n,seq,d=1,*x.shape[1:]
    g=w.shape[0]
    w3=qkv.shape[2]//g
    lw=w3//3
    img=pl.BlockSpec((1,seq,d),lambda i,t:(i,0,0))
    return pl.pallas_call(attn_bwd_kernel,grid=(n,g),
        in_specs=[pl.BlockSpec((1,seq,w3),lambda i,t:(i,0,t)),pl.BlockSpec((1,seq,lw),lambda i,t:(i,0,t)),
            pl.BlockSpec((1,d,w3),lambda i,t:(t,0,0)),pl.BlockSpec((1,seq,d),lambda i,t:(at,0,0)),img,row(d)],
        out_specs=[pl.BlockSpec((1,seq,w3),lambda i,t:(i,0,t)),pl.BlockSpec((1,1,2,lw),lambda i,t:(i,t,0,0)),img,pl.BlockSpec((1,2,d),lambda i,t:(i,0,0))],
        out_shape=[jax.ShapeDtypeStruct((n,seq,g*w3),BF),jax.ShapeDtypeStruct((n,g,2,lw),F32),jax.ShapeDtypeStruct((n,seq,d),BF),jax.ShapeDtypeStruct((n,2,d),F32)],
        scratch_shapes=[pltpu.VMEM((seq,d),F32)],
        **params("attn_bwd",2*n*seq*d*g*w3+40*n*seq*seq*g*lw,n*seq*(2*g*w3+g*lw+4*d)*2+g*w3*d*2,n*g*lw//HD*seq*seq))(qkv,do,w,x,dres,gain)


def cut(total,out_ref):
    out_ref[...]=total.astype(BF).reshape(out_ref.shape)

def image_sum(refs):
    n=len(refs)//2
    return sum(dot(l[0],r[0],TN) for l,r in zip(refs[:n],refs[n:]))

def grad_kernel(*refs):
    cut(image_sum(refs[:-1]),refs[-1])

def grad_fc1_kernel(*refs):
    out_ref=refs[-1]
    half=len(refs)//2
    n_dp,_,rows,width=out_ref.shape
    fw=refs[half-1].shape[2]
    lw=width-fw
    out_ref[:,0,:,:fw]=image_sum(refs[:half]).astype(BF).reshape(n_dp,rows,fw)
    proj=image_sum(refs[half:-1]).astype(BF)
    per=lw//rows
    for b in range(n_dp//per):
        out_ref[b*per:(b+1)*per,0,:,fw:]=proj[:,b*lw:(b+1)*lw].reshape(per,rows,lw)

def shard_grads(kernel,name,n_dp,g,rows,width,specs,ops):
    return pl.pallas_call(kernel,
        grid=(g,),in_specs=specs,out_specs=pl.BlockSpec((n_dp,1,rows//n_dp,width),lambda k:(0,k,0,0)),
        out_shape=jax.ShapeDtypeStruct((n_dp,g,rows//n_dp,width),BF),
        **params(name,0,0))(*ops)

def whole(ops): return [pl.BlockSpec((1,*a.shape[1:]),lambda k:(0,0,0)) for a in ops]

def both(a): return [pl.BlockSpec((1,*a.shape[1:]),lambda k,i=i:(i,0,0)) for i in range(a.shape[0])]

def part(ops,g): return [pl.BlockSpec((1,a.shape[1],a.shape[2]//g),lambda k:(0,0,k)) for a in ops]

def grad_fc2(hid,cot,n_dp,g):
    ff,d=hid[0].shape[2],cot.shape[2]
    return shard_grads(grad_kernel,"grad_fc2",n_dp,g,ff//g,d,part(hid,g)+both(cot),(*hid,*[cot]*len(hid)))

def grad_fc1(act,dpre,att,dres,n_dp,g):
    ff,d=dpre[0].shape[2],act[0].shape[2]
    return shard_grads(grad_fc1_kernel,"grad_fc1",n_dp,g,d,ff//g+d//g,
        whole(act)+part(dpre,g)+part(att,g)+whole(dres),(*act,*dpre,*att,*dres))

def grad_qkv(act,dqkv,n_dp,g):
    w,d=dqkv[0].shape[2],act[0].shape[2]
    return shard_grads(grad_kernel,"grad_qkv",n_dp,g,d,w//g,whole(act)+part(dqkv,g),(*act,*dqkv))

def interleave(rows,out_ref):
    out_ref[...]=jnp.swapaxes(jnp.stack([r.astype(F32) for r in rows],axis=0),0,1).astype(BF)

def weave_kernel(*refs):
    interleave([ref[t] for t in range(refs[0].shape[0]) for ref in refs[:-1]],refs[-1])

def weave(parts,tile=64):
    n_t,seq,d=parts[0].shape
    n=n_t*len(parts)
    out=pl.pallas_call(weave_kernel,grid=(pl.cdiv(seq,tile),),
        in_specs=[pl.BlockSpec((n_t,tile,d),lambda r:(0,r,0))]*len(parts),
        out_specs=pl.BlockSpec((tile,n,d),lambda r:(r,0,0)),
        out_shape=jax.ShapeDtypeStruct((seq,n,d),BF),**params("weave",0,0))(*parts)
    return out.transpose(1,0,2)

def adamw(weight_old, moment_one, moment_two, grad_sum, rate_value, decay_value):
    new_one = BETA_ONE * moment_one + (1.0 - BETA_ONE) * grad_sum
    new_two = BETA_TWO * moment_two + (1.0 - BETA_TWO) * grad_sum * grad_sum
    one_hat = new_one / (1.0 - BETA_ONE**STEP)
    two_hat = new_two / (1.0 - BETA_TWO**STEP)
    new_weight = weight_old - rate_value * (
        one_hat / (jnp.sqrt(two_hat) + ADAM_EPS) + decay_value * weight_old
    )
    return (new_weight, new_one, new_two)


def shift(value, axis, by):
    n = lax.axis_size(axis)
    return lax.ppermute(value, axis, [(i, (i + by) % n) for i in range(n)])


def swap(value, axis, mask):
    n = lax.axis_size(axis)
    return lax.ppermute(value, axis, [(i, i ^ mask) for i in range(n)])


def spread_moves(bufs, c, p, units, target):
    half = units * p // 2
    moves = []
    for flip, buf in enumerate(bufs):
        base = c ^ flip
        for at, slot in enumerate((base, base ^ 2, base ^ 4)):
            first = pl.multiple_of(slot * p, p)
            moves += [(buf.at[pl.ds((at * units + k) * p, p)], target(k, first, p)) for k in range(units)]
        first = pl.multiple_of((base ^ 6) * p, p)
        moves += [(buf.at[pl.ds((3 * units + k) * p, p)], target(k, first, p)) for k in range(units)]
    return moves


def run_copies(moves, sems):
    copies = [pltpu.make_async_copy(src, dst, sems.at[i]) for i, (src, dst) in enumerate(moves)]
    for copy in copies:
        copy.start()
    for copy in copies:
        copy.wait()


def place_kernel(at_ref, own_ref, near_ref, far_ref, out_ref, sems):
    p = near_ref.shape[0] // 12
    moves = spread_moves((near_ref, far_ref), at_ref[0], p, 3, lambda k, first, n: out_ref.at[k + 1, pl.ds(first, n)])
    run_copies([(own_ref, out_ref.at[0])] + moves, sems)


def spread_kernel(at_ref, near_ref, far_ref, out_ref, sems):
    p = near_ref.shape[0] // 4
    run_copies(spread_moves((near_ref, far_ref), at_ref[0], p, 1, lambda k, first, n: out_ref.at[pl.ds(first, n)]), sems)


def dma_call(kernel, name, n, out_shape, ops):
    at = lax.axis_index("dp").reshape(1).astype(jnp.int32)
    return pl.pallas_call(
        kernel,
        in_specs=[pl.BlockSpec(memory_space=pltpu.SMEM)] + [pl.BlockSpec(memory_space=pltpu.VMEM)] * len(ops),
        out_specs=pl.BlockSpec(memory_space=pl.ANY),
        out_shape=out_shape,
        scratch_shapes=[pltpu.SemaphoreType.DMA((n,))],
        **params(name, 0, 0),
    )(at, *ops)


def after(value, *earlier):
    return lax.optimization_barrier((value, *earlier))[0]


def tie(*values):
    return lax.optimization_barrier(values)


def shards(piece):
    return [shift(piece, "tensor", k) for k in range(1, lax.axis_size("tensor"))]


def fetch(mine):
    if lax.axis_size("dp") != 8:
        return mine, mine
    return swap(mine, "dp", 2), swap(mine, "dp", 4)


def fetch_diagonal(xs, ys):
    half = xs.shape[0] // 2
    if lax.axis_size("dp") != 8:
        return xs[:half], ys[half:]
    return swap(xs[:half], "dp", 4), swap(ys[half:], "dp", 2)


def finish(own, mine, xs, ys, da, db, name):
    if lax.axis_size("dp") != 8:
        every = lax.all_gather(mine.reshape(lax.axis_size("tensor") - 1, -1, own.shape[1]), "dp", axis=1, tiled=True)
        return jnp.concatenate([own[None], every], 0)
    near = jnp.concatenate([mine, xs, ys, da, db], 0)
    shape = jax.ShapeDtypeStruct((4, *own.shape), own.dtype)
    return dma_call(place_kernel, name, 25, shape, (own, near, swap(near, "dp", 1)))


def reduce_dp(parts):
    return lax.psum_scatter(parts, "dp", scatter_dimension=0, tiled=False)


def parts_of(value):
    parts = []
    for _ in range(3):
        parts.append(lax.reduce_precision(value, 8, 7))
        value = value - parts[-1]
    return [v.astype(BF) for v in parts]


def sum_chain(value):
    for axis in ("tensor", "dp"):
        mask = 1
        while mask < lax.axis_size(axis):
            value = value + (yield swap(value, axis, mask))
            mask *= 2
    return value


def reduce_chain(part, name):
    n_t = part.shape[0]
    up, down = part[1], part[n_t - 1]
    for step in range(1, n_t):
        up, down = yield (
            lax.ppermute(up, "tensor", [(i, i + 1) for i in range(step)]),
            lax.ppermute(down, "tensor", [(n_t - 1 - i, n_t - 2 - i) for i in range(step)]),
        )
        if step < n_t - 1:
            up = (up.astype(F32) + part[step + 1].astype(F32)).astype(BF)
            down = (down.astype(F32) + part[n_t - 1 - step].astype(F32)).astype(BF)
    mine = (part[0].astype(F32) + up.astype(F32) + down.astype(F32)).astype(BF)
    if lax.axis_size("dp") != 8:
        return lax.all_gather(mine, "dp", axis=0, tiled=True).astype(F32)
    xs, ys = yield fetch(mine)
    da, db = yield fetch_diagonal(xs, ys)
    near = jnp.concatenate([mine, xs, ys, da, db], 0)
    far = yield swap(near, "dp", 1)
    shape = jax.ShapeDtypeStruct((8 * mine.shape[0], mine.shape[1]), mine.dtype)
    return dma_call(spread_kernel, name, 8, shape, (near, far)).astype(F32)


def run_chains(chains, work, made):
    live, results, step = {}, [None] * len(chains), 0
    while step == 0 or live or work or any(begin >= step for begin, _ in chains):
        moved = {}
        for at, (begin, make) in enumerate(chains):
            if begin == step:
                live[at] = make()
                moved[at] = next(live[at])
            elif at in live:
                try:
                    moved[at] = live[at].send(kept[at])
                except StopIteration as end:
                    results[at] = end.value
                    del live[at]
        if work:
            made.append(work.pop(0)(made, results))
            moved, made[-1] = tie(moved, made[-1])
        else:
            moved = tie(moved)[0]
        kept = moved
        step += 1
    return results


def per_device(*args):
    tokens, cotangent = args[0], args[1]
    weights, firsts, seconds = args[2:10], args[10:18], args[18:26]
    qkv_weight, qv_bias, proj_weight, fc1_weight, fc1_bias, fc2_weight, norm_gains, shift_biases = weights
    n_t = lax.axis_size("tensor")
    n_dp = lax.axis_size("dp")
    t_at = lax.axis_index("tensor")
    dp_at = lax.axis_index("dp")
    width = tokens.shape[2]
    own = tokens.shape[0] // n_t
    lw = qkv_weight.shape[2]
    fw = fc1_weight.shape[1]

    def proj_pack(value):
        return value.reshape(lw, n_t, lw).transpose(1, 0, 2).reshape(width, lw)

    def proj_unpack(value):
        return value.reshape(n_t, lw, lw).transpose(1, 0, 2).reshape(lw, width)

    mix = jnp.concatenate([qkv_weight[:, 0], qkv_weight[:, 1], qkv_weight[:, 2], proj_pack(proj_weight)], axis=1)
    p = width // n_dp
    mix = mix.astype(BF)
    biases = jnp.concatenate([qv_bias.reshape(-1), fc1_bias])
    flat = jnp.concatenate(parts_of(biases))
    columns = mix.shape[1]
    extra = 16 * pl.cdiv(flat.size, 16 * columns)
    flat = jnp.pad(flat, (0, extra * columns - flat.size)).reshape(extra, columns)

    def dp_rows(w):
        return lax.dynamic_slice_in_dim(w, dp_at * (w.shape[0] // n_dp), w.shape[0] // n_dp, 0).astype(BF)

    rows = dp_rows(qkv_weight)
    proj_rows = lax.dynamic_slice(proj_weight, (dp_at * p % lw, dp_at * p // lw * lw), (p, lw)).astype(BF)
    p0 = jnp.concatenate([rows[:, 0], rows[:, 1], rows[:, 2], proj_rows], axis=1)
    p1, p2 = dp_rows(fc1_weight), dp_rows(fc2_weight)
    z0 = shards(jnp.concatenate([p0, flat], axis=0))
    x = lax.dynamic_slice_in_dim(tokens, t_at * own, own, 0)
    cot = lax.dynamic_slice_in_dim(cotangent, t_at * own, own, 0)
    fc1, fc2 = fc1_weight.astype(BF), fc2_weight.astype(BF)
    z0, x, cot, fc1, fc2, p1, p2 = tie(z0, x, cot, fc1, fc2, p1, p2)
    mine0 = jnp.concatenate([z[:p] for z in z0], 0)
    near0, z1 = fetch(mine0), shards(p1)
    near0, z1, p2 = tie(near0, z1, p2)
    mine1 = jnp.concatenate(z1, 0)
    diag0, near1, z2 = fetch_diagonal(*near0), fetch(mine1), shards(p2)
    diag0, near1, z2 = tie(diag0, near1, z2)
    mine2 = jnp.concatenate(z2, 0)
    w_mix = finish(mix, mine0, *near0, *diag0, name="place_mix")
    diag1, near2 = fetch_diagonal(*near1), fetch(mine2)
    flat = jnp.stack([z[p:].reshape(-1)[: 3 * biases.size].astype(F32).reshape(3, -1) for z in z0])
    bias_rel = jnp.concatenate([biases[None], flat[:, 0] + flat[:, 1] + flat[:, 2]], axis=0)
    qv_rel = bias_rel[:, : 2 * lw].reshape(n_t, 2, lw)
    qkv_bias = jnp.stack([qv_rel[:, 0], jnp.zeros_like(qv_rel[:, 0]), qv_rel[:, 1]], axis=1).reshape(n_t, 3 * lw)
    b1_rel = bias_rel[:, 2 * lw :].reshape(-1)
    gain1, gain2 = norm_gains[0:1], norm_gains[1:2]

    def gather(mine):
        return lax.all_gather(mine[0], "tensor", axis=0, tiled=False)

    act1, qkv, attended = [], [], []
    resid, act2, hidden, slope, out_all = [], [], [], [], []
    for i in range(own):
        made = qkv_attn(i, after(x, *hidden[-1:]), gain1, shift_biases[0:1], w_mix, qkv_bias)
        for kept, value in zip((act1, qkv, attended), made):
            kept.append(value)
        if i == 0:
            diag1, near2, head = tie(diag1, near2, attended[0])
            diag2 = fetch_diagonal(*near2)
            w_fc1 = finish(after(fc1, head), mine1, *near1, *diag1, name="place_fc1")
            w_fc1, diag2 = tie(w_fc1, diag2)
            w_fc2 = finish(fc2, mine2, *near2, *diag2, name="place_fc2")
        *kept, out_own = mlp_fwd(
            i, x, attended[i], w_mix, shift_biases[2:3], gain2, shift_biases[1:2], w_fc1, b1_rel, w_fc2, shift_biases[3:4]
        )
        for made, value in zip((resid, act2, hidden, slope), kept):
            made.append(value)
        out_all.append(gather(out_own))
    g_fc2 = grad_fc2(hidden, cot, n_dp, n_t)
    slope[0] = after(slope[0], g_fc2)
    part_fc2 = reduce_dp(g_fc2)
    d_pre, g_b1, d_resid, d_resid_b, d_att, sums2 = [], [], [], [], [], []
    for i in range(own):
        made = mlp_bwd(i, cot, after(slope[i], *d_pre[-1:]), w_fc2, w_fc1, resid[i], gain2, w_mix)
        for kept, value in zip((d_pre, g_b1, d_resid, d_resid_b, d_att, sums2), made):
            kept.append(value)
    part_fc1 = grad_fc1(act2, d_pre, attended, d_resid_b, n_dp, n_t)
    part_fc1, *d_att = tie(part_fc1, *d_att)
    part_fc1 = reduce_dp(part_fc1)
    d_att[0], out_all[0], part_fc2 = tie(d_att[0], out_all[0], part_fc2)
    gt_all = [None] * own

    def attention_back(i):
        def run(made, results):
            d = after(d_att[i], *(made[-1] if made else ()))
            if i == own - 1:
                d, out_all[i] = tie(d, out_all[i])
            dq, gq, gt_own, s1 = attn_bwd(i, qkv[i], d, w_mix, x, d_resid[i], gain1)
            gt_all[i] = gather(gt_own)
            return dq, gq, s1

        return run

    def attention_grad(made, results):
        return grad_qkv(act1, [m[0] for m in made], n_dp, n_t)

    rates = (
        1.2 / math.sqrt(D),
        0.6,
        0.6 / math.sqrt(max(D // 128, 1)),
        0.6 / math.sqrt(D),
        0.3,
        0.6 / math.sqrt(max(FF // 8, 1)),
        3.0,
        3.0,
    )
    decays = (MATRIX_DECAY, 0.0, MATRIX_DECAY, MATRIX_DECAY, 0.0, MATRIX_DECAY, 0.0, 0.0)

    def step(at, grad):
        return adamw(weights[at], firsts[at], seconds[at], grad, rates[at], decays[at])

    order = (t_at + n_t - jnp.arange(n_t)) % n_t

    def vectors():
        _, g_qv, sums1 = (sum(v[1:], v[0]) for v in zip(*made[:own]))
        rel = jnp.concatenate([g_qv.reshape(n_t, -1), sum(g_b1).reshape(n_t, -1)], axis=1)
        rel = jnp.take(rel, order, axis=0)
        return jnp.concatenate([rel.reshape(-1), sums1.reshape(-1), sum(sums2).reshape(-1)])

    def fc2_step(made, results):
        return results[1], step(5, results[1])

    def fc1_step(made, results):
        g_fc1, g_proj = results[2][:, :fw], proj_unpack(results[2][:, fw:])
        return g_fc1, g_proj, step(3, g_fc1), step(2, g_proj)

    def waits_for(i):
        return lambda made, results: gt_all[i]

    def nothing(made, results):
        return ()

    made = []
    chains = [
        (own + 1, lambda: sum_chain(vectors())),
        (own, lambda: reduce_chain(part_fc2, "spread_fc2")),
        (own + 1, lambda: reduce_chain(part_fc1, "spread_fc1")),
        (own + 3, lambda: reduce_chain(reduce_dp(made[own]), "spread_qkv")),
    ]
    work = [attention_back(i) for i in range(own)] + [
        attention_grad,
        lambda made, results: weave(out_all),
        waits_for(0),
        nothing,
        nothing,
        nothing,
        nothing if n_t > 4 else fc2_step,
        nothing if n_t > 4 else fc1_step,
        waits_for(-1),
    ]
    flat, g_fc2, g_fc1, g_qkv = run_chains(chains, work, made)
    output, grad_tokens = made[own + 1], weave(gt_all[:-1] + [made[-1]])
    if n_t > 4:
        made[own + 6], made[own + 7] = fc2_step(made, (None, g_fc2)), fc1_step(made, (None, None, g_fc1))
    (g_fc2, new_fc2), (g_fc1, g_proj, new_fc1, new_proj) = made[own + 6], made[own + 7]
    rel = 2 * lw + fw
    g_qkv = jnp.stack([g_qkv[:, i * lw : (i + 1) * lw] for i in range(3)], axis=1)
    mine = lax.dynamic_index_in_dim(flat[: n_t * rel].reshape(n_t, rel), t_at, 0, keepdims=False)
    rest = flat[n_t * rel :].reshape(6, width)
    g_gains = jnp.stack([rest[0], rest[2]])
    g_shifts = jnp.stack([rest[1], rest[3], rest[4], rest[5]])
    grads = (g_qkv, mine[: 2 * lw].reshape(2, lw), g_proj, g_fc1, mine[2 * lw :], g_fc2, g_gains, g_shifts)
    updated = [step(at, grad) for at, grad in enumerate(grads)]
    updated[3], updated[5], updated[2] = new_fc1, new_fc2, new_proj
    return (
        output,
        grad_tokens,
        *grads,
        *(u[0] for u in updated),
        *(u[1] for u in updated),
        *(u[2] for u in updated),
    )


def solution(mesh):
    weights = (
        P(None, None, "tensor"),
        P(None, "tensor"),
        P("tensor", None),
        P(None, "tensor"),
        P("tensor"),
        P("tensor", None),
        P(),
        P(),
    )
    images = (P("dp", None, None), P("dp", None, None))
    return jax.shard_map(
        per_device,
        mesh=mesh,
        in_specs=images + weights * 3,
        out_specs=images + weights * 4,
        check_vma=False,
    )
```
